128 devices in a mesh: dp: 32 (over y, x_hi, z), tensor: 4 (over x_lo, core).
Axes of the slice: x: 4 (x_hi: 2, x_lo: 2; x = x_hi * 2 + x_lo), y: 4, z: 4, core: 2. Of those that a mesh axis runs over, the one named last changes fastest.
Arguments:
- hidden_in: bfloat16 [32, 512, 4096], P('dp', None, 'tensor'), may hold values from -6 to 6
- norm_gain: bfloat16 [4096], replicated, may hold values from 0.25 to 1.75
- w_query: bfloat16 [4096, 4096], P('dp', 'tensor'), may hold values from -0.09375 to 0.09375
- w_key: bfloat16 [4096, 1024], P('dp', 'tensor'), may hold values from -0.09375 to 0.09375
- w_value: bfloat16 [4096, 1024], P('dp', 'tensor'), may hold values from -0.09375 to 0.09375
- w_out: bfloat16 [4096, 4096], P('tensor', 'dp'), may hold values from -0.09375 to 0.09375
- final_gain: bfloat16 [4096], P('tensor'), may hold values from 0.25 to 1.75
- latents: bfloat16 [512, 4096], P(None, 'tensor'), may hold values from -200 to 200
- token_mask: int32 [32, 512], P('dp'), may hold values from 0 to 1, as said below
- queries: bfloat16 [65536, 4096], P('dp', 'tensor'), may hold values from -6 to 6
Outputs:
- similarity_matrix: float32 [65536, 32], P('dp')
- log_norm: float32 [65536], P('dp')
The draws below stay inside these ranges and needn't reach their ends.
Inputs may be any that keep to these rules, and one draw needn't show every extreme that they name: `token_mask`: in each passage the mask is 1 on a leading run of at least 64 tokens and 0 after it; the first passage has no padding.
All inputs are finite; a program needn't handle non-finite values.
Results may differ from the reference program's by a relative error of at most 0.015.
Values may be sent and summed in bfloat16 or wider, within the bound.
No kernel may reach another device: no remote copies, remote signals or barrier semaphores. Data moves between devices by JAX's collectives and lax.ppermute only.
A program may use at most 128 MiB of HBM per device.

```python
import jax
import jax.numpy as jnp
from jax import lax

D = 4096
HEADS = 32
KV_HEADS = 8
HEAD = 128
LATENTS = 512
LEN = 512
PASSAGES = 32
QUERIES = 65536


def draw_latents(key, part):
    key = jax.random.fold_in(key, 7)
    base = jax.random.normal(key, (LATENTS, D), jnp.float32)
    base = jnp.clip(base, -6.0, 6.0)
    return base.astype(jnp.bfloat16)


def draw_token_mask(key, part):
    key = jax.random.fold_in(key, 3)
    lengths = jax.random.randint(key, (PASSAGES, 1), LEN // 8, LEN + 1)
    lengths = lengths.at[0, 0].set(LEN)
    sequence_indices = jnp.arange(LEN, dtype=jnp.int32)[None, :]
    return (sequence_indices < lengths).astype(jnp.int32)


def steps_of(own_key, extent, shards, smallest, top_value):
    gain, own = 1.0, jax.random.fold_in(own_key, 6)
    for dim, parts in shards:
        steps = jnp.exp(jax.random.uniform(jax.random.fold_in(own, dim), (parts,), jnp.float32, smallest / len(shards), top_value / len(shards)))
        gain = gain * jnp.repeat(steps, extent[dim] // parts).reshape([-1 if axis == dim else 1 for axis in range(len(extent))])
    return gain


def bell_draw(own_key, shape, spread, bound, pieces=(), kind=jnp.bfloat16):
    drawn = jax.random.normal(own_key, shape, jnp.float32) * spread
    if len(pieces) > 0:
        drawn = steps_of(own_key, shape, pieces, -0.22, 0.18) * drawn
    return jnp.clip(drawn, min=-bound, max=bound).astype(kind)


def setup_inputs(seed: int = 0) -> dict:
    arg_keys = jax.random.split(jax.random.key(seed), 11)
    return {
        "hidden_in": bell_draw(arg_keys[0], (PASSAGES, LEN, D), 1.0, 6.0, ((0, 32), (2, 4))),
        "norm_gain": jnp.clip(1.0 + 0.15 * jax.random.normal(arg_keys[1], (D,), jnp.float32), 0.25, 1.75).astype(jnp.bfloat16),
        "w_query": bell_draw(arg_keys[2], (D, D), D ** -0.5, 0.09375, ((0, 32), (1, 4))),
        "w_key": bell_draw(arg_keys[3], (D, KV_HEADS * HEAD), D ** -0.5, 0.09375, ((0, 32), (1, 4))),
        "w_value": bell_draw(arg_keys[4], (D, KV_HEADS * HEAD), D ** -0.5, 0.09375, ((0, 32), (1, 4))),
        "w_out": bell_draw(arg_keys[5], (D, D), D ** -0.5, 0.09375, ((0, 4), (1, 32))),
        "final_gain": jnp.clip(1.0 + 0.15 * jax.random.normal(arg_keys[6], (D,), jnp.float32), 0.25, 1.75).astype(jnp.bfloat16),
        "latents": draw_latents(jax.random.fold_in(arg_keys[10], 71), 0),
        "token_mask": draw_token_mask(jax.random.fold_in(arg_keys[10], 71), 0),
        "queries": bell_draw(arg_keys[9], (QUERIES, D), 1.0, 6.0, ((0, 32), (1, 4))),
    }


EPS = 1e-05
logit_divisor = 0.02

def apply_rotary(values, sequence_indices):
    half = values.shape[-1] // 2
    freqs = 10000.0 ** (-2.0 * jnp.arange(half, dtype=jnp.float32) / values.shape[-1])
    angle = sequence_indices[:, None] * freqs[None, :]
    cosine = jnp.cos(angle)[:, None, :]
    sine = jnp.sin(angle)[:, None, :]
    first = values[..., :half]
    second = values[..., half:]
    return jnp.concatenate([first * cosine - second * sine, second * cosine + first * sine], axis=-1)

def reference(hidden_in, norm_gain, w_query, w_key, w_value, w_out, final_gain, latents, token_mask, queries):
    group = HEADS // KV_HEADS
    scale = HEAD ** (-0.5)
    sequence_indices = jnp.arange(LEN, dtype=jnp.float32)
    lat_f = latents.astype(jnp.float32).reshape(LATENTS, HEADS, HEAD)

    def one(pair):
        tokens, mask = pair
        full_f = tokens.astype(jnp.float32)
        normed = (full_f * lax.rsqrt(lax.optimization_barrier(jnp.mean(full_f * full_f, -1, keepdims=True)) + EPS) * norm_gain.astype(jnp.float32)).astype(jnp.bfloat16)
        query = jnp.dot(normed, w_query, preferred_element_type=jnp.float32)
        key = jnp.dot(normed, w_key, preferred_element_type=jnp.float32)
        value = jnp.dot(normed, w_value, preferred_element_type=jnp.float32)
        q_rot = apply_rotary(query.reshape(LEN, HEADS, HEAD), sequence_indices).astype(jnp.bfloat16).reshape(LEN, KV_HEADS, group, HEAD)
        k_rot = apply_rotary(key.reshape(LEN, KV_HEADS, HEAD), sequence_indices).astype(jnp.bfloat16)
        v_half = value.astype(jnp.bfloat16).reshape(LEN, KV_HEADS, HEAD)
        logits = jnp.einsum('qgrd,kgd->grqk', q_rot.astype(jnp.float32), k_rot.astype(jnp.float32)) * scale
        logits = jnp.where(mask[None, None, None, :] > 0, logits, -1e+30)
        attention_weights = jax.nn.softmax(logits, axis=-1).astype(jnp.bfloat16)
        attended_values = jnp.einsum('grqk,kgd->qgrd', attention_weights.astype(jnp.float32), v_half.astype(jnp.float32))
        attended_values = attended_values.astype(jnp.bfloat16).reshape(LEN, D)
        h_new = (full_f + jnp.dot(attended_values, w_out, preferred_element_type=jnp.float32)).astype(jnp.bfloat16)
        h_f = h_new.astype(jnp.float32)
        hn = (h_f * lax.rsqrt(lax.optimization_barrier(jnp.mean(h_f * h_f, -1, keepdims=True)) + EPS) * final_gain.astype(jnp.float32)).astype(jnp.bfloat16)
        hn_f = hn.astype(jnp.float32)
        cross_logits = jnp.einsum('qhd,khd->hqk', hn_f.reshape(LEN, HEADS, HEAD), lat_f) * scale
        latent_cross_weights = jax.nn.softmax(cross_logits, axis=-1).astype(jnp.bfloat16)
        cross = jnp.einsum('hqk,khd->qhd', latent_cross_weights.astype(jnp.float32), lat_f).reshape(LEN, D)
        mask_f = mask.astype(jnp.float32)
        summed = lax.optimization_barrier(jnp.sum((hn_f + cross) * mask_f[:, None], axis=0))
        return summed / jnp.sum(mask_f)
    pooled = lax.map(one, (hidden_in, token_mask))
    embedding = (pooled * lax.rsqrt(lax.optimization_barrier(jnp.sum(pooled * pooled, -1, keepdims=True)) + 1e-06)).astype(jnp.bfloat16)
    inner_product_matrix = jnp.dot(queries, embedding.T, preferred_element_type=jnp.float32)
    q_f = queries.astype(jnp.float32)
    question_norm_sq = lax.optimization_barrier(jnp.sum(q_f * q_f, -1))
    similarity_matrix = inner_product_matrix * lax.rsqrt(question_norm_sq + 1e-06)[:, None] / logit_divisor
    log_norm = jax.nn.logsumexp(similarity_matrix, axis=1)
    return (similarity_matrix, log_norm)
```

```python
import jax
import jax.numpy as jnp
from jax import lax
from jax.sharding import PartitionSpec as P

HEAD = 128
EPS = 1e-05
logit_divisor = 0.02
BOTH = ("dp", "tensor")
COORDS = [
    (y, a, z, b, c)
    for y in range(4)
    for a in range(2)
    for z in range(4)
    for b in range(2)
    for c in range(2)
]


def index_of(y, a, z, b, c):
    return (((y * 2 + a) * 4 + z) * 2 + b) * 2 + c


def move(values, where):
    pairs = [(index_of(*at), index_of(*where(*at))) for at in COORDS]
    return lax.ppermute(values, BOTH, pairs)


def swap_core(values):
    return move(values, lambda y, a, z, b, c: (y, a, z, b, 1 - c))


def along_x(step):
    def where(y, a, z, b, c):
        x = (2 * a + b + step) % 4
        return (y, x // 2, z, x % 2, c)

    return where


def first_leg(step):
    def where(y, a, z, b, c):
        if c == 0:
            return ((y + step) % 4, a, z, b, c)
        return (y, a, (z + step) % 4, b, c)

    return where


def second_leg(step):
    def where(y, a, z, b, c):
        if c == 0:
            return (y, a, (z + step) % 4, b, c)
        return ((y + step) % 4, a, z, b, c)

    return where


def ring(values, leg):
    half = values.shape[0] // 2
    before = move(values, leg(1))
    after = move(values, leg(-1))
    far_low = move(before[:half], leg(1))
    far_high = move(after[half:], leg(-1))
    return values, before, after, jnp.concatenate([far_low, far_high], axis=0)


def apply_rotary(values, sequence_indices):
    half = values.shape[-1] // 2
    freqs = 10000.0 ** (-2.0 * jnp.arange(half, dtype=jnp.float32) / values.shape[-1])
    angle = sequence_indices[:, None] * freqs[None, :]
    cosine = jnp.cos(angle)[None, :, None, :]
    sine = jnp.sin(angle)[None, :, None, :]
    first = values[..., :half]
    second = values[..., half:]
    return jnp.concatenate(
        [first * cosine - second * sine, second * cosine + first * sine], axis=-1
    )


def place_blocks(blocks, position):
    out = jnp.zeros((4,) + blocks[0].shape, blocks[0].dtype)
    for block, offset in zip(blocks, (0, 3, 1, 2), strict=True):
        at = (position + offset) % 4
        out = lax.dynamic_update_slice(out, block[None], (at,) + (0,) * block.ndim)
    return out


def local(
    hidden_in, norm_gain, w_query, w_key, w_value, w_out, final_gain, latents, token_mask, queries
):
    length, part_width = hidden_in.shape[1:]
    width = norm_gain.shape[0]
    scale = HEAD ** (-0.5)
    dp, tensor = lax.axis_index("dp"), lax.axis_index("tensor")
    y, x_hi, z = dp // 8, (dp // 4) % 2, dp % 4
    x_lo, core = tensor // 2, tensor % 2
    x = 2 * x_hi + x_lo
    leg1 = jnp.where(core == 0, y, z)
    leg2 = jnp.where(core == 0, z, y)

    def halves(weights, part):
        wide = weights.shape[1] // 2
        return lax.dynamic_slice_in_dim(weights, part * wide, wide, 1)

    mine = jnp.concatenate([halves(w, x_hi) for w in (w_query, w_key, w_value)], axis=1)
    other = jnp.concatenate([halves(w, 1 - x_hi) for w in (w_query, w_key, w_value)], axis=1)
    other = move(other, lambda y, a, z, b, c: (y, 1 - a, z, b, c))
    low = jnp.where(x_hi == 0, mine, other)
    high = jnp.where(x_hi == 0, other, mine)
    shard = jnp.stack([low, high])
    line = place_blocks(ring(shard, first_leg), leg1)
    grid = place_blocks(ring(line, second_leg), leg2)
    w_all = jnp.where(core == 0, grid.transpose(1, 2, 0, 3, 4), grid.transpose(0, 2, 1, 3, 4))
    w_all = w_all.reshape(width, -1)

    own = hidden_in[0]

    def over_x(values):
        near = ring(values, along_x)
        return [(block, swap_core(block)) for block in near]

    def by_core(pair):
        return (
            jnp.where(core == 0, pair[0], pair[1]),
            jnp.where(core == 0, pair[1], pair[0]),
        )

    tokens = place_blocks([jnp.stack(by_core(pair)) for pair in over_x(own)], x)
    tokens = tokens.reshape(2, 2, 2, length, part_width).transpose(0, 3, 1, 2, 4)
    tokens = tokens.reshape(2 * length, width)
    tokens_f = tokens.astype(jnp.float32)
    normed = (
        tokens_f
        * lax.rsqrt(jnp.mean(tokens_f * tokens_f, -1, keepdims=True) + EPS)
        * norm_gain.astype(jnp.float32)
    ).astype(jnp.bfloat16)
    normed = lax.optimization_barrier(normed)
    qkv = jnp.dot(normed, w_all, preferred_element_type=jnp.float32)
    heads = (qkv.shape[1] // HEAD) - 2
    qkv = qkv.reshape(2, length, heads + 2, HEAD)
    sequence_indices = jnp.arange(length, dtype=jnp.float32)
    q_rot = apply_rotary(qkv[:, :, :heads], sequence_indices).astype(jnp.bfloat16)
    k_rot = apply_rotary(qkv[:, :, heads : heads + 1], sequence_indices).astype(jnp.bfloat16)
    value = qkv[:, :, heads + 1].astype(jnp.bfloat16)
    mask_other = move(token_mask, lambda y, a, z, b, c: (y, 1 - a, z, b, c))
    mask = jnp.concatenate(
        [
            jnp.where(x_hi == 0, token_mask, mask_other),
            jnp.where(x_hi == 0, mask_other, token_mask),
        ],
        axis=0,
    )
    logits = (
        jnp.einsum("pqrd,pkd->prqk", q_rot, k_rot[:, :, 0], preferred_element_type=jnp.float32)
        * scale
    )
    logits = jnp.where(mask[:, None, None, :] > 0, logits, -1e30)
    weights = jax.nn.softmax(logits, axis=-1).astype(jnp.bfloat16)
    attended = jnp.einsum("prqk,pkd->pqrd", weights, value, preferred_element_type=jnp.float32)
    attended = attended.astype(jnp.bfloat16).reshape(2 * length, heads * HEAD)

    block = move(w_out, lambda y, a, z, b, c: (2 * b + c, a, z, y // 2, y % 2))
    out_line = place_blocks(ring(block, first_leg), leg1)
    out_grid = place_blocks(ring(out_line, second_leg), leg2)
    w_out_all = jnp.where(
        core == 0, out_grid.transpose(1, 2, 0, 3), out_grid.transpose(0, 2, 1, 3)
    ).reshape(width, -1)
    gathered = place_blocks([jnp.stack(by_core(pair)) for pair in over_x(attended)], x)
    gathered = gathered.reshape((2, 2, 2) + attended.shape).transpose(3, 1, 2, 0, 4)
    gathered = gathered.reshape(2 * length, width)
    product = jnp.dot(gathered, w_out_all, preferred_element_type=jnp.float32)
    part = product.shape[1]
    start = tensor * part_width + x_hi * part
    h = lax.dynamic_slice_in_dim(tokens, start, part, 1).astype(jnp.float32) + product
    h = h.astype(jnp.bfloat16).astype(jnp.float32)
    square = jnp.sum(h * h, -1)
    square = square + swap_core(square)
    square = square + move(square, lambda y, a, z, b, c: (y, a, z, 1 - b, c))
    square = square + move(square, lambda y, a, z, b, c: (y, 1 - a, z, b, c))
    gain = lax.dynamic_slice_in_dim(final_gain, x_hi * part, part, 0).astype(jnp.float32)
    hn = (h * lax.rsqrt(square[:, None] / width + EPS) * gain).astype(jnp.bfloat16)
    lat = lax.dynamic_slice_in_dim(latents, x_hi * part, part, 1)
    lat_heads = lat.reshape(lat.shape[0], heads, HEAD)
    hn_heads = hn.reshape(2 * length, heads, HEAD)
    cross_logits = (
        jnp.einsum("qhd,khd->hqk", hn_heads, lat_heads, preferred_element_type=jnp.float32) * scale
    )
    cross_weights = jax.nn.softmax(cross_logits, axis=-1).astype(jnp.bfloat16)
    cross = jnp.einsum(
        "hqk,khd->qhd", cross_weights, lat_heads, preferred_element_type=jnp.float32
    )
    mixed = (hn.astype(jnp.float32) + cross.reshape(2 * length, part)).reshape(2, length, part)
    mask_f = mask.astype(jnp.float32)
    pooled = jnp.sum(mixed * mask_f[:, :, None], axis=1) / jnp.sum(mask_f, axis=1, keepdims=True)

    sums = jnp.sum(pooled * pooled, -1, keepdims=True)
    emb = pooled.astype(jnp.bfloat16)[None, :, None, None]

    def gather4(values, axis, position):
        def where(step):
            def to(y, a, z, b, c):
                if axis == 0:
                    return ((y + step) % 4, a, z, b, c)
                return (y, a, (z + step) % 4, b, c)

            return to

        parts = [values] + [move(values, where(step)) for step in (1, 2, 3)]
        out = jnp.zeros(values.shape[:axis] + (4,) + values.shape[axis + 1 :], values.dtype)
        for step, piece in enumerate(parts):
            at = [0] * values.ndim
            at[axis] = (position - step) % 4
            out = lax.dynamic_update_slice(out, piece, at)
        return out

    emb = gather4(emb, 0, y)
    emb = gather4(emb, 2, z)
    emb_other = move(emb, lambda y, a, z, b, c: (y, 1 - a, z, b, c))
    emb = jnp.concatenate(
        [jnp.where(x_hi == 0, emb, emb_other), jnp.where(x_hi == 0, emb_other, emb)], axis=3
    )
    every = emb.reshape(32, part_width)
    every_f = every.astype(jnp.float32)
    square_e = jnp.sum(every_f * every_f, -1)
    del sums
    products = lax.dot_general(
        every, queries, (((1,), (1,)), ((), ())), preferred_element_type=jnp.float32
    )
    products = jnp.concatenate([products, jnp.broadcast_to(square_e[:, None], (32, HEAD))], axis=1)

    def over_tensor(values):
        values = values + swap_core(values)
        return values + move(values, lambda y, a, z, b, c: (y, a, z, 1 - b, c))

    q_f = queries.astype(jnp.float32)
    question_norm_sq = over_tensor(jnp.sum(q_f * q_f, -1))
    products = over_tensor(products)
    count = queries.shape[0]
    similarity = (
        products[:, :count]
        * lax.rsqrt(products[:, count : count + 1] + 1e-06)
        * lax.rsqrt(question_norm_sq + 1e-06)[None, :]
        / logit_divisor
    )
    log_norm = jax.nn.logsumexp(similarity, axis=0)
    return (similarity.T, log_norm)


def solution(mesh):
    placed = (
        P("dp", None, "tensor"),
        P(),
        P("dp", "tensor"),
        P("dp", "tensor"),
        P("dp", "tensor"),
        P("tensor", "dp"),
        P("tensor"),
        P(None, "tensor"),
        P("dp", None),
        P("dp", "tensor"),
    )
    return jax.shard_map(
        local, mesh=mesh, in_specs=placed, out_specs=(P("dp", None), P("dp")), check_vma=False
    )
```

```python
import jax
import jax.numpy as jnp
from jax import lax
from jax.experimental import pallas as pl
from jax.experimental.pallas import tpu as pltpu
from jax.sharding import PartitionSpec as P

HEAD = 128
EPS = 1e-05
logit_divisor = 0.02
BOTH = ("dp", "tensor")
COORDS = [
    (y, a, z, b, c)
    for y in range(4)
    for a in range(2)
    for z in range(4)
    for b in range(2)
    for c in range(2)
]


def index_of(y, a, z, b, c):
    return (((y * 2 + a) * 4 + z) * 2 + b) * 2 + c


def move(values, where):
    pairs = [(index_of(*at), index_of(*where(*at))) for at in COORDS]
    return lax.ppermute(values, BOTH, pairs)


def swap_core(values):
    return move(values, lambda y, a, z, b, c: (y, a, z, b, 1 - c))


def along_x(step):
    def where(y, a, z, b, c):
        x = (2 * a + b + step) % 4
        return (y, x // 2, z, x % 2, c)

    return where


def first_leg(step):
    def where(y, a, z, b, c):
        if c == 0:
            return ((y + step) % 4, a, z, b, c)
        return (y, a, (z + step) % 4, b, c)

    return where


def second_leg(step):
    def where(y, a, z, b, c):
        if c == 0:
            return (y, a, (z + step) % 4, b, c)
        return ((y + step) % 4, a, z, b, c)

    return where


def swap_x_hi(values):
    return move(values, lambda y, a, z, b, c: (y, 1 - a, z, b, c))


def swap_x_lo(values):
    return move(values, lambda y, a, z, b, c: (y, a, z, 1 - b, c))


def ring(values, leg):
    half = values.shape[0] // 2
    before = move(values, leg(1))
    after = move(values, leg(-1))
    far_low = move(before[:half], leg(1))
    far_high = move(after[half:], leg(-1))
    return values, before, after, far_low, far_high


def over_x(values):
    blocks = ring(values, along_x)
    return tuple(blocks) + tuple(swap_core(block) for block in blocks)


AT_Y, AT_X_HI, AT_Z, AT_X_LO, AT_CORE, AT_PASSAGE = range(6)
VMEM = pl.BlockSpec(memory_space=pltpu.VMEM)
SMEM = pl.BlockSpec(memory_space=pltpu.SMEM)
ANY = pl.BlockSpec(memory_space=pl.ANY)
F32, BF16 = jnp.float32, jnp.bfloat16
OFFSETS = (0, 3, 1, 2)
NT = (((1,), (1,)), ((), ()))
EXPONENT = HEAD ** (-0.5) * 1.4426950408889634


def call(kernel, args, specs, out, scratch, flops, nbytes, exps=0):
    return pl.pallas_call(
        kernel,
        out_shape=out,
        in_specs=specs,
        out_specs=jax.tree.map(lambda _: VMEM, out),
        scratch_shapes=scratch,
        compiler_params=pltpu.CompilerParams(vmem_limit_bytes=48 * 1024 * 1024),
        cost_estimate=pl.CostEstimate(flops=flops, bytes_accessed=nbytes, transcendentals=exps),
    )(*args)


def by_x(at, source, passage):
    chip = (2 * at[AT_X_HI] + at[AT_X_LO] + source) % 4
    return chip // 2, chip % 2


def norm_kernel(at, *refs):
    own, before, after, low, high, own2, before2, after2, low2, high2 = refs[:10]
    gain, out, tokens, sems = refs[10:]
    rows, part = own.shape
    half = rows // 2
    passage, core = at[AT_PASSAGE], at[AT_CORE]
    here = at[AT_X_HI] == passage
    near = (2 * passage + 1 - at[AT_X_LO] - 2 * at[AT_X_HI] - at[AT_X_LO] + 4) % 4
    for k, (mine, first, second, ahead, behind) in enumerate(
        ((own, low, high, after, before), (own2, low2, high2, after2, before2))
    ):
        there = core if k == 0 else 1 - core
        col = pl.multiple_of((2 * at[AT_X_LO] + there) * part, part)
        col2 = pl.multiple_of((2 * (1 - at[AT_X_LO]) + there) * part, part)

        def send(src, lo, count, column, sem):
            return pltpu.make_async_copy(
                src, tokens.at[pl.ds(lo, count), pl.ds(column, part)], sems.at[sem]
            )

        @pl.when(here)
        def _():
            send(mine.at[pl.ds(0, half)], 0, half, col, 3 * k).start()
            send(mine.at[pl.ds(half, half)], half, half, col, 3 * k + 1).start()

        @pl.when(jnp.logical_not(here))
        def _():
            send(first, 0, half, col, 3 * k).start()
            send(second, half, half, col, 3 * k + 1).start()

        @pl.when(near == 1)
        def _():
            send(ahead, 0, rows, col2, 3 * k + 2).start()

        @pl.when(near != 1)
        def _():
            send(behind, 0, rows, col2, 3 * k + 2).start()

    for k, (first, ahead) in enumerate(((low, after), (low2, after2))):
        send(first, 0, half, 0, 3 * k).wait()
        send(first, half, half, 0, 3 * k + 1).wait()
        send(ahead, 0, rows, 0, 3 * k + 2).wait()

    width = tokens.shape[1]

    @pl.loop(0, rows // 16)
    def _(step):
        at_rows = pl.ds(pl.multiple_of(step * 16, 16), 16)
        block = tokens[at_rows, :].astype(F32)
        mean = jnp.sum(block * block, axis=-1, keepdims=True) / width
        out[at_rows, :] = (block * lax.rsqrt(mean + EPS) * gain[...].astype(F32)).astype(BF16)


def normalize(at, pieces, gain):
    rows, part = pieces[0].shape
    width = gain.shape[1]
    return call(
        norm_kernel,
        (at, *pieces, gain),
        [SMEM] + [ANY] * 10 + [VMEM],
        jax.ShapeDtypeStruct((rows, width), BF16),
        [pltpu.VMEM((rows, width), BF16), pltpu.SemaphoreType.DMA((6,))],
        8 * rows * width,
        4 * rows * width,
    )


def leg_positions(at, first, second):
    p1 = jnp.where(at[AT_CORE] == 0, at[AT_Y], at[AT_Z])
    p2 = jnp.where(at[AT_CORE] == 0, at[AT_Z], at[AT_Y])
    p1, p2 = (p1 + first) % 4, (p2 + second) % 4
    return jnp.where(at[AT_CORE] == 0, p1, p2), jnp.where(at[AT_CORE] == 0, p2, p1)


def grid_copies(at, pieces, sems, per_line, target):
    copies = []
    for two, second in enumerate(OFFSETS):
        for one, first in enumerate(OFFSETS):
            if two < 3:
                piece, place = pieces[two], one
            else:
                piece, place = pieces[3 + one // 2], one % 2
            y, z = leg_positions(at, first, second)
            for entry in range(per_line):
                src, dst = target(piece, place, y, z, entry)
                copies.append(pltpu.make_async_copy(src, dst, sems.at[len(copies)]))
    return copies


def attention_kernel(at, normed, w0, w1, w2, w3, w4, cosine, sine, bias, out, weights, qkv, sems):
    rows = normed.shape[0]
    heads = out.shape[1] // HEAD
    deep = 128

    def target(piece, place, y, z, entry):
        row = (y * 8 + (at[AT_X_HI] + entry) % 2 * 4 + z) * deep
        return (
            piece.at[pl.ds((2 * place + entry) * deep, deep)],
            weights.at[pl.ds(pl.multiple_of(row, deep), deep)],
        )

    copies = grid_copies(at, (w0, w1, w2, w3, w4), sems, 2, target)
    for copy in copies:
        copy.start()
    for copy in copies:
        copy.wait()

    tile = 128

    @pl.loop(0, rows // tile)
    def _(step):
        at_rows = pl.ds(pl.multiple_of(step * tile, tile), tile)
        product = jnp.dot(normed[at_rows, :], weights[...], preferred_element_type=F32)
        cos, sin = cosine[at_rows, :], sine[at_rows, :]
        for head in range(heads + 1):
            block = product[:, head * HEAD : (head + 1) * HEAD]
            turned = block * cos + pltpu.roll(block, HEAD // 2, 1) * sin
            qkv[at_rows, head * HEAD : (head + 1) * HEAD] = turned.astype(BF16)
        qkv[at_rows, (heads + 1) * HEAD :] = product[:, (heads + 1) * HEAD :].astype(BF16)

    keys = qkv[:, heads * HEAD : (heads + 1) * HEAD]
    values_t = qkv[:, (heads + 1) * HEAD :].astype(F32).T.astype(BF16)
    for head in range(heads):
        query = qkv[:, head * HEAD : (head + 1) * HEAD]
        logits = lax.dot_general(keys, query, NT, preferred_element_type=F32)
        logits = logits + bias[...]
        top = jnp.max(logits, axis=0, keepdims=True)
        power = jnp.exp2((logits - top) * EXPONENT)
        total = jnp.sum(power, axis=0, keepdims=True)
        mixed = jnp.dot(values_t, power.astype(BF16), preferred_element_type=F32)
        out[:, head * HEAD : (head + 1) * HEAD] = (mixed / total).T.astype(BF16)


def attend(at, normed, pieces, cosine, sine, bias):
    rows, width = normed.shape
    wide = pieces[0].shape[1]
    heads = wide // HEAD - 2
    return call(
        attention_kernel,
        (at, normed, *pieces, cosine, sine, bias),
        [SMEM, VMEM] + [ANY] * 5 + [VMEM] * 3,
        jax.ShapeDtypeStruct((rows, heads * HEAD), BF16),
        [
            pltpu.VMEM((width, wide), BF16),
            pltpu.VMEM((rows, wide), BF16),
            pltpu.SemaphoreType.DMA((32,)),
        ],
        2 * rows * width * wide + 4 * heads * rows * rows * HEAD,
        2 * (rows * width + width * wide),
        heads * rows * rows,
    )


def output_kernel(at, *refs):
    pieces, blocks, (own, low, high) = refs[:10], refs[10:15], refs[15:18]
    h, square, full, weights, residual, sems, w_sems, r_sems = refs[18:]
    rows, part = pieces[0].shape
    half = rows // 2
    passage = at[AT_PASSAGE]

    def target(piece, place, y, z, entry):
        count = weights.shape[0] // 4
        return (
            piece.at[pl.ds(place * count, count)],
            weights.at[
                pl.ds(pl.multiple_of(y * count, count), count),
                pl.ds(pl.multiple_of(z * HEAD, HEAD), HEAD),
            ],
        )

    copies = grid_copies(at, blocks, w_sems, 1, target)
    for k, piece in enumerate(pieces):
        source = (0, 3, 1, 2, 2)[k % 5]
        chip = (2 * at[AT_X_HI] + at[AT_X_LO] + source) % 4
        there = at[AT_CORE] if k < 5 else 1 - at[AT_CORE]
        column = ((chip % 2 * 2 + there) * 2 + chip // 2) * part
        lo = half if k % 5 == 4 else 0
        copies.append(
            pltpu.make_async_copy(
                piece,
                full.at[pl.ds(lo, piece.shape[0]), pl.ds(pl.multiple_of(column, part), part)],
                sems.at[k],
            )
        )
    for copy in copies:
        copy.start()
    columns = pl.ds(pl.multiple_of(at[AT_X_HI] * part, part), part)
    here = at[AT_X_HI] == passage

    def keep(src, lo, sem):
        return pltpu.make_async_copy(
            src.at[:, columns], residual.at[pl.ds(lo, half)], r_sems.at[sem]
        )

    @pl.when(here)
    def _():
        keep(own.at[pl.ds(0, half)], 0, 0).start()
        keep(own.at[pl.ds(half, half)], half, 1).start()

    @pl.when(jnp.logical_not(here))
    def _():
        keep(low, 0, 0).start()
        keep(high, half, 1).start()

    keep(low, 0, 0).wait()
    keep(high, half, 1).wait()
    for copy in copies:
        copy.wait()

    tile = 128
    for step in range(rows // tile):
        at_rows = slice(step * tile, (step + 1) * tile)
        product = jnp.dot(full[at_rows, :], weights[...], preferred_element_type=F32)
        block = (residual[at_rows, :].astype(F32) + product).astype(BF16)
        h[at_rows, :] = block
        block = block.astype(F32)
        block = block * block
        folded = block[:, :HEAD]
        for k in range(1, part // HEAD):
            folded = folded + block[:, k * HEAD : (k + 1) * HEAD]
        square[:, at_rows] = jnp.sum(folded.T, axis=0, keepdims=True)


def project(at, pieces, blocks, hidden):
    rows, part = pieces[0].shape
    width = 8 * part
    return call(
        output_kernel,
        (at, *pieces, *blocks, *hidden),
        [SMEM] + [ANY] * 18,
        (jax.ShapeDtypeStruct((rows, part), BF16), jax.ShapeDtypeStruct((1, rows), F32)),
        [
            pltpu.VMEM((rows, width), BF16),
            pltpu.VMEM((width, part), BF16),
            pltpu.VMEM((rows, part), BF16),
            pltpu.SemaphoreType.DMA((10,)),
            pltpu.SemaphoreType.DMA((16,)),
            pltpu.SemaphoreType.DMA((2,)),
        ],
        2 * rows * width * part,
        2 * (rows * width + width * part),
    )


def pool_kernel(width, at, h, square, gain, latents, mask, out, hn):
    rows, part = h.shape
    entries = latents.shape[0]
    columns = pl.ds(pl.multiple_of(at[AT_X_HI] * part, part), part)
    scale = jnp.broadcast_to(lax.rsqrt(square[...] / width + EPS), (HEAD, rows)).T
    keep = jnp.broadcast_to(mask[...], (HEAD, rows)).T
    count = jnp.sum(mask[...], axis=1, keepdims=True)
    own_gain = gain[:, columns].astype(F32)
    for head in range(part // HEAD):
        cols = slice(head * HEAD, (head + 1) * HEAD)
        block = (h[:, cols].astype(F32) * scale * own_gain[:, cols]).astype(BF16)
        lat = latents[:, pl.ds(pl.multiple_of(at[AT_X_HI] * part + head * HEAD, HEAD), HEAD)]
        logits = lax.dot_general(lat, block, NT, preferred_element_type=F32)
        top = jnp.max(logits, axis=0, keepdims=True)
        power = jnp.exp2((logits - top) * EXPONENT)
        share = mask[...] / jnp.sum(power, axis=0, keepdims=True)
        power = power * share
        folded = power[:, :HEAD]
        for k in range(1, rows // HEAD):
            folded = folded + power[:, k * HEAD : (k + 1) * HEAD]
        taken = jnp.sum(folded, axis=1, keepdims=True)
        cross = jnp.sum(taken * lat.astype(F32), axis=0, keepdims=True)
        kept = jnp.sum(block.astype(F32) * keep, axis=0, keepdims=True)
        out[:, cols] = (cross + kept) / count


def pool(at, h, square, gain, latents, mask):
    rows, part = h.shape
    width = 8 * part
    entries = latents.shape[0]

    def kernel(*refs):
        pool_kernel(width, *refs)

    return call(
        kernel,
        (at, h, square, gain, latents, mask),
        [SMEM] + [VMEM] * 5,
        jax.ShapeDtypeStruct((1, part), F32),
        [pltpu.VMEM((rows, part), BF16)],
        2 * rows * part * entries,
        2 * (rows * part + 2 * entries * part),
        4 * rows * entries,
    )


def local(
    hidden_in, norm_gain, w_query, w_key, w_value, w_out, final_gain, latents, token_mask, queries
):
    length, part_width = hidden_in.shape[1:]
    dp, tensor = lax.axis_index("dp"), lax.axis_index("tensor")
    y, x_hi, z = dp // 8, (dp // 4) % 2, dp % 4
    x_lo, core = tensor // 2, tensor % 2

    def table(passage):
        return jnp.stack([y, x_hi, z, x_lo, core, jnp.int32(passage)]).astype(jnp.int32)

    def halves(weights, part):
        wide = weights.shape[1] // 2
        return lax.dynamic_slice_in_dim(weights, part * wide, wide, 1)

    own = hidden_in[0]
    hidden = over_x(own)

    mine = jnp.concatenate([halves(w, x_hi) for w in (w_query, w_key, w_value)], axis=1)
    other = jnp.concatenate([halves(w, 1 - x_hi) for w in (w_query, w_key, w_value)], axis=1)
    shard = jnp.concatenate([mine, swap_x_hi(other)], axis=0)
    line = jnp.concatenate(ring(shard, first_leg), axis=0)
    w_pieces = ring(line, second_leg)

    block = move(w_out, lambda y, a, z, b, c: (2 * b + c, a, z, y // 2, y % 2))
    out_line = jnp.concatenate(ring(block, first_leg), axis=0)
    out_pieces = ring(out_line, second_leg)

    mask_other = swap_x_hi(token_mask)
    masks = (
        jnp.where(x_hi == 0, token_mask, mask_other).astype(F32),
        jnp.where(x_hi == 0, mask_other, token_mask).astype(F32),
    )
    half = HEAD // 2
    freqs = 10000.0 ** (-2.0 * jnp.arange(half, dtype=F32) / HEAD)
    angle = jnp.arange(length, dtype=F32)[:, None] * freqs[None, :]
    cosine = jnp.concatenate([jnp.cos(angle), jnp.cos(angle)], axis=1)
    sine = jnp.concatenate([-jnp.sin(angle), jnp.sin(angle)], axis=1)

    q_f = queries.astype(F32)
    question_norm_sq = jnp.sum(q_f * q_f, -1)
    question_norm_sq = question_norm_sq + swap_core(question_norm_sq)
    question_norm_sq = question_norm_sq + swap_x_lo(question_norm_sq)

    pooled = []
    for passage in range(2):
        at = table(passage)
        normed = normalize(at, hidden, norm_gain[None])
        bias = jnp.where(masks[passage][0][:, None] > 0, 0.0, -1e30).astype(F32)
        bias = jnp.broadcast_to(bias, (length, length))
        attended = attend(at, normed, w_pieces, cosine, sine, bias)
        gathered = over_x(attended)
        h, square = project(at, gathered, out_pieces, (own, hidden[3], hidden[4]))
        square = square + swap_core(square)
        square = square + swap_x_lo(square)
        square = square + swap_x_hi(square)
        pooled.append(pool(at, h, square, final_gain[None], latents, masks[passage]))

    emb = jnp.concatenate(pooled, axis=0).astype(BF16)
    part = emb.shape[1]
    emb_other = swap_x_hi(emb)
    emb = jnp.concatenate(
        [jnp.where(x_hi == 0, emb, emb_other), jnp.where(x_hi == 0, emb_other, emb)], axis=1
    )

    def gather4(values, axis, position):
        def where(step):
            def to(y, a, z, b, c):
                if axis == 0:
                    return ((y + step) % 4, a, z, b, c)
                return (y, a, (z + step) % 4, b, c)

            return to

        parts = [values] + [move(values, where(step)) for step in (1, 2, 3)]
        out = jnp.zeros(values.shape[:axis] + (4,) + values.shape[axis + 1 :], values.dtype)
        for step, piece in enumerate(parts):
            at = [0] * values.ndim
            at[axis] = (position - step) % 4
            out = lax.dynamic_update_slice(out, piece, at)
        return out

    emb = emb[None, :, None]
    emb = gather4(gather4(emb, 2, z), 0, y)
    every = emb.reshape(32, part_width)
    every_f = every.astype(F32)
    square_e = jnp.sum(every_f * every_f, -1)
    products = lax.dot_general(every, queries, NT, preferred_element_type=F32)
    products = jnp.concatenate([products, jnp.broadcast_to(square_e[:, None], (32, HEAD))], axis=1)
    products = products + swap_core(products)
    products = products + swap_x_lo(products)
    count = queries.shape[0]
    similarity = (
        products[:, :count]
        * lax.rsqrt(products[:, count : count + 1] + 1e-06)
        * lax.rsqrt(question_norm_sq + 1e-06)[None, :]
        / logit_divisor
    )
    log_norm = jax.nn.logsumexp(similarity, axis=0)
    return (similarity.T, log_norm)


def solution(mesh):
    placed = (
        P("dp", None, "tensor"),
        P(),
        P("dp", "tensor"),
        P("dp", "tensor"),
        P("dp", "tensor"),
        P("tensor", "dp"),
        P("tensor"),
        P(None, "tensor"),
        P("dp", None),
        P("dp", "tensor"),
    )
    return jax.shard_map(
        local, mesh=mesh, in_specs=placed, out_specs=(P("dp", None), P("dp")), check_vma=False
    )
```

```python
import jax
import jax.numpy as jnp
from jax import lax
from jax.experimental import pallas as pl
from jax.experimental.pallas import tpu as pltpu
from jax.sharding import PartitionSpec as P

HEAD = 128
EPS = 1e-05
logit_divisor = 0.02
BOTH = ("dp", "tensor")
COORDS = [
    (y, a, z, b, c)
    for y in range(4)
    for a in range(2)
    for z in range(4)
    for b in range(2)
    for c in range(2)
]


def index_of(y, a, z, b, c):
    return (((y * 2 + a) * 4 + z) * 2 + b) * 2 + c


def move(values, where):
    pairs = [(index_of(*at), index_of(*where(*at))) for at in COORDS]
    return lax.ppermute(values, BOTH, pairs)


def swap_core(values):
    return move(values, lambda y, a, z, b, c: (y, a, z, b, 1 - c))


def along_x(step):
    def where(y, a, z, b, c):
        x = (2 * a + b + step) % 4
        return (y, x // 2, z, x % 2, c)

    return where


def first_leg(step):
    def where(y, a, z, b, c):
        if c == 0:
            return ((y + step) % 4, a, z, b, c)
        return (y, a, (z + step) % 4, b, c)

    return where


def second_leg(step):
    def where(y, a, z, b, c):
        if c == 0:
            return (y, a, (z + step) % 4, b, c)
        return ((y + step) % 4, a, z, b, c)

    return where


def swap_x_hi(values):
    return move(values, lambda y, a, z, b, c: (y, 1 - a, z, b, c))


def swap_x_lo(values):
    return move(values, lambda y, a, z, b, c: (y, a, z, 1 - b, c))


def ring(values, leg):
    half = values.shape[0] // 2
    before = move(values, leg(1))
    after = move(values, leg(-1))
    far_low = move(before[:half], leg(1))
    far_high = move(after[half:], leg(-1))
    return values, before, after, far_low, far_high


def direct(values, leg):
    return values, move(values, leg(1)), move(values, leg(-1)), move(values, leg(2))


def over_x(values):
    blocks = ring(values, along_x)
    return tuple(blocks) + tuple(swap_core(block) for block in blocks)


def behind(values, *others):
    return lax.optimization_barrier((values,) + others)[0]


AT_Y, AT_X_HI, AT_Z, AT_X_LO, AT_CORE, AT_PASSAGE = range(6)
VMEM = pl.BlockSpec(memory_space=pltpu.VMEM)
SMEM = pl.BlockSpec(memory_space=pltpu.SMEM)
ANY = pl.BlockSpec(memory_space=pl.ANY)
F32, BF16 = jnp.float32, jnp.bfloat16
OFFSETS = (0, 3, 1, 2)
NT = (((1,), (1,)), ((), ()))
EXPONENT = HEAD ** (-0.5) * 1.4426950408889634


def call(kernel, args, specs, out, scratch, flops, nbytes, exps=0):
    return pl.pallas_call(
        kernel,
        out_shape=out,
        in_specs=specs,
        out_specs=jax.tree.map(lambda _: VMEM, out),
        scratch_shapes=scratch,
        compiler_params=pltpu.CompilerParams(vmem_limit_bytes=48 * 1024 * 1024),
        cost_estimate=pl.CostEstimate(flops=flops, bytes_accessed=nbytes, transcendentals=exps),
    )(*args)


def by_x(at, source, passage):
    chip = (2 * at[AT_X_HI] + at[AT_X_LO] + source) % 4
    return chip // 2, chip % 2


def norm_kernel(at, *refs):
    own, before, after, low, high, own2, before2, after2, low2, high2 = refs[:10]
    gain, out, tokens, sems = refs[10:]
    rows, part = own.shape
    half = rows // 2
    passage, core = at[AT_PASSAGE], at[AT_CORE]
    here = at[AT_X_HI] == passage
    near = (2 * passage + 1 - at[AT_X_LO] - 2 * at[AT_X_HI] - at[AT_X_LO] + 4) % 4
    for k, (mine, first, second, ahead, behind) in enumerate(
        ((own, low, high, after, before), (own2, low2, high2, after2, before2))
    ):
        there = core if k == 0 else 1 - core
        col = pl.multiple_of((2 * at[AT_X_LO] + there) * part, part)
        col2 = pl.multiple_of((2 * (1 - at[AT_X_LO]) + there) * part, part)

        def send(src, lo, count, column, sem):
            return pltpu.make_async_copy(
                src, tokens.at[pl.ds(lo, count), pl.ds(column, part)], sems.at[sem]
            )

        @pl.when(here)
        def _():
            send(mine.at[pl.ds(0, half)], 0, half, col, 3 * k).start()
            send(mine.at[pl.ds(half, half)], half, half, col, 3 * k + 1).start()

        @pl.when(jnp.logical_not(here))
        def _():
            send(first, 0, half, col, 3 * k).start()
            send(second, half, half, col, 3 * k + 1).start()

        @pl.when(near == 1)
        def _():
            send(ahead, 0, rows, col2, 3 * k + 2).start()

        @pl.when(near != 1)
        def _():
            send(behind, 0, rows, col2, 3 * k + 2).start()

    for k, (first, ahead) in enumerate(((low, after), (low2, after2))):
        send(first, 0, half, 0, 3 * k).wait()
        send(first, half, half, 0, 3 * k + 1).wait()
        send(ahead, 0, rows, 0, 3 * k + 2).wait()

    width = tokens.shape[1]
    tile = 64

    @pl.loop(0, rows // tile)
    def _(step):
        at_rows = pl.ds(pl.multiple_of(step * tile, tile), tile)
        total = jnp.zeros((tile, HEAD), F32)
        for lane in range(0, width, HEAD):
            block = tokens[at_rows, lane : lane + HEAD].astype(F32)
            total = total + block * block
        mean = jnp.sum(total, axis=-1, keepdims=True) / width
        scale = jnp.broadcast_to(lax.rsqrt(mean + EPS), (tile, HEAD))
        for lane in range(0, width, HEAD):
            block = tokens[at_rows, lane : lane + HEAD].astype(F32)
            own_gain = gain[:, lane : lane + HEAD].astype(F32)
            out[at_rows, lane : lane + HEAD] = (block * scale * own_gain).astype(BF16)


def normalize(at, pieces, gain):
    rows, part = pieces[0].shape
    width = gain.shape[1]
    return call(
        norm_kernel,
        (at, *pieces, gain),
        [SMEM] + [ANY] * 10 + [VMEM],
        jax.ShapeDtypeStruct((rows, width), BF16),
        [pltpu.VMEM((rows, width), BF16), pltpu.SemaphoreType.DMA((6,))],
        8 * rows * width,
        4 * rows * width,
    )


def leg_positions(at, first, second):
    p1 = jnp.where(at[AT_CORE] == 0, at[AT_Y], at[AT_Z])
    p2 = jnp.where(at[AT_CORE] == 0, at[AT_Z], at[AT_Y])
    p1, p2 = (p1 + first) % 4, (p2 + second) % 4
    return jnp.where(at[AT_CORE] == 0, p1, p2), jnp.where(at[AT_CORE] == 0, p2, p1)


def attention_kernel(at, *refs):
    source, pieces, (cosine, sine, bias, out) = refs[0], refs[1:11], refs[11:15]
    normed, weights, total, qkv, sems = refs[15:]
    rows = normed.shape[0]
    heads = out.shape[1] // HEAD
    line = pieces[0].shape[0]
    half = line // 2
    deep = line // 4
    copies = [pltpu.make_async_copy(source, normed, sems.at[0])]
    waits = [[copies[0]], [], [], []]
    for two in range(4):
        for entry in range(2):
            row = (2 * two + entry) * line
            group = pieces[5 * entry : 5 * entry + 5]
            blocks = [(group[two], row)] if two < 3 else [(group[3], row), (group[4], row + half)]
            for piece, lo in blocks:
                copy = pltpu.make_async_copy(
                    piece, weights.at[pl.ds(lo, piece.shape[0])], sems.at[len(copies)]
                )
                copies.append(copy)
                waits[two].append(copy)
    for copy in copies:
        copy.start()
    for two, second in enumerate(OFFSETS):
        for copy in waits[two]:
            copy.wait()
        taken = []
        for entry in range(2):
            for first in OFFSETS:
                y, z = leg_positions(at, first, second)
                row = (y * 8 + (at[AT_X_HI] + entry) % 2 * 4 + z) * deep
                taken.append(normed[:, pl.ds(pl.multiple_of(row, deep), deep)])
        product = jnp.dot(
            jnp.concatenate(taken, axis=1),
            weights[2 * two * line : 2 * (two + 1) * line, :],
            preferred_element_type=F32,
        )
        total[...] = product if two == 0 else total[...] + product

    for head in range(heads + 1):
        cols = slice(head * HEAD, (head + 1) * HEAD)
        block = total[:, cols]
        turned = block * cosine[...] + pltpu.roll(block, HEAD // 2, 1) * sine[...]
        qkv[:, cols] = turned.astype(BF16)
    keys = qkv[:, heads * HEAD : (heads + 1) * HEAD]
    values_t = total[:, (heads + 1) * HEAD :].T.astype(BF16)
    for head in range(heads):
        query = qkv[:, head * HEAD : (head + 1) * HEAD]
        logits = lax.dot_general(keys, query, NT, preferred_element_type=F32)
        logits = logits + jnp.concatenate([bias[...]] * (rows // HEAD), axis=1)
        top = jnp.max(logits, axis=0, keepdims=True)
        power = jnp.exp2((logits - top) * EXPONENT)
        share = 1.0 / jnp.sum(power, axis=0, keepdims=True)
        mixed = jnp.dot(values_t, power.astype(BF16), preferred_element_type=F32)
        out[:, head * HEAD : (head + 1) * HEAD] = (mixed * share).T.astype(BF16)


def attend(at, normed, pieces, cosine, sine, bias):
    rows, width = normed.shape
    wide = pieces[0].shape[1]
    heads = wide // HEAD - 2
    return call(
        attention_kernel,
        (at, normed, *pieces, cosine, sine, bias),
        [SMEM] + [ANY] * 11 + [VMEM] * 3,
        jax.ShapeDtypeStruct((rows, heads * HEAD), BF16),
        [
            pltpu.VMEM((rows, width), BF16),
            pltpu.VMEM((width, wide), BF16),
            pltpu.VMEM((rows, wide), F32),
            pltpu.VMEM((rows, wide), BF16),
            pltpu.SemaphoreType.DMA((11,)),
        ],
        2 * rows * width * wide + 4 * heads * rows * rows * HEAD,
        2 * (rows * width + width * wide),
        heads * rows * rows,
    )


def output_kernel(at, *refs):
    pieces, blocks, (own, low, high) = refs[:10], refs[10:14], refs[14:17]
    h, square, full, weights, residual, sems, w_sems, r_sems = refs[17:]
    rows, part = pieces[0].shape
    half = rows // 2
    count = weights.shape[0] // 4
    passage = at[AT_PASSAGE]
    copies = []
    for two, second in enumerate(OFFSETS):
        for one, first in enumerate(OFFSETS):
            y, z = leg_positions(at, first, second)
            copies.append(
                pltpu.make_async_copy(
                    blocks[two].at[pl.ds(one * count, count)],
                    weights.at[
                        pl.ds(pl.multiple_of(y * count, count), count),
                        pl.ds(pl.multiple_of(z * HEAD, HEAD), HEAD),
                    ],
                    w_sems.at[4 * two + one],
                )
            )
    for k, piece in enumerate(pieces):
        source = (0, 3, 1, 2, 2)[k % 5]
        chip = (2 * at[AT_X_HI] + at[AT_X_LO] + source) % 4
        there = at[AT_CORE] if k < 5 else 1 - at[AT_CORE]
        column = ((chip % 2 * 2 + there) * 2 + chip // 2) * part
        lo = half if k % 5 == 4 else 0
        copies.append(
            pltpu.make_async_copy(
                piece,
                full.at[pl.ds(lo, piece.shape[0]), pl.ds(pl.multiple_of(column, part), part)],
                sems.at[k],
            )
        )
    for copy in copies:
        copy.start()
    columns = pl.ds(pl.multiple_of(at[AT_X_HI] * part, part), part)
    here = at[AT_X_HI] == passage

    def keep(src, lo, sem):
        return pltpu.make_async_copy(
            src.at[:, columns], residual.at[pl.ds(lo, half)], r_sems.at[sem]
        )

    @pl.when(here)
    def _():
        keep(own.at[pl.ds(0, half)], 0, 0).start()
        keep(own.at[pl.ds(half, half)], half, 1).start()

    @pl.when(jnp.logical_not(here))
    def _():
        keep(low, 0, 0).start()
        keep(high, half, 1).start()

    keep(low, 0, 0).wait()
    keep(high, half, 1).wait()
    for copy in copies:
        copy.wait()

    folded = jnp.zeros((rows, HEAD), F32)
    wide = 256
    for lane in range(0, part, wide):
        cols = slice(lane, lane + wide)
        product = jnp.dot(full[...], weights[:, cols], preferred_element_type=F32)
        block = (residual[:, cols].astype(F32) + product).astype(BF16)
        h[:, cols] = block
        block = block.astype(F32)
        block = block * block
        for k in range(0, wide, HEAD):
            folded = folded + block[:, k : k + HEAD]
    square[...] = jnp.sum(folded.T, axis=0, keepdims=True)


def project(at, pieces, blocks, hidden):
    rows, part = pieces[0].shape
    width = 8 * part
    return call(
        output_kernel,
        (at, *pieces, *blocks, *hidden),
        [SMEM] + [ANY] * 17,
        (jax.ShapeDtypeStruct((rows, part), BF16), jax.ShapeDtypeStruct((1, rows), F32)),
        [
            pltpu.VMEM((rows, width), BF16),
            pltpu.VMEM((width, part), BF16),
            pltpu.VMEM((rows, part), BF16),
            pltpu.SemaphoreType.DMA((10,)),
            pltpu.SemaphoreType.DMA((16,)),
            pltpu.SemaphoreType.DMA((2,)),
        ],
        2 * rows * width * part,
        2 * (rows * width + width * part),
    )


def pool_kernel(width, at, h, square, gain, latents, mask, out, hn):
    rows, part = h.shape
    entries = latents.shape[0]
    columns = pl.ds(pl.multiple_of(at[AT_X_HI] * part, part), part)
    scale = jnp.broadcast_to(lax.rsqrt(square[...] / width + EPS), (HEAD, rows)).T
    keep = jnp.broadcast_to(mask[...], (HEAD, rows)).T
    count = jnp.sum(mask[...], axis=1, keepdims=True)
    own_gain = gain[:, columns].astype(F32)
    for head in range(part // HEAD):
        cols = slice(head * HEAD, (head + 1) * HEAD)
        block = (h[:, cols].astype(F32) * scale * own_gain[:, cols]).astype(BF16)
        lat = latents[:, pl.ds(pl.multiple_of(at[AT_X_HI] * part + head * HEAD, HEAD), HEAD)]
        logits = lax.dot_general(lat, block, NT, preferred_element_type=F32)
        top = jnp.max(logits, axis=0, keepdims=True)
        power = jnp.exp2((logits - top) * EXPONENT)
        share = mask[...] / jnp.sum(power, axis=0, keepdims=True)
        power = power * share
        folded = power[:, :HEAD]
        for k in range(1, rows // HEAD):
            folded = folded + power[:, k * HEAD : (k + 1) * HEAD]
        taken = jnp.sum(folded, axis=1, keepdims=True)
        cross = jnp.sum(taken * lat.astype(F32), axis=0, keepdims=True)
        kept = jnp.sum(block.astype(F32) * keep, axis=0, keepdims=True)
        out[:, cols] = (cross + kept) / count


def pool(at, h, square, gain, latents, mask):
    rows, part = h.shape
    width = 8 * part
    entries = latents.shape[0]

    def kernel(*refs):
        pool_kernel(width, *refs)

    return call(
        kernel,
        (at, h, square, gain, latents, mask),
        [SMEM] + [VMEM] * 5,
        jax.ShapeDtypeStruct((1, part), F32),
        [pltpu.VMEM((rows, part), BF16)],
        2 * rows * part * entries,
        2 * (rows * part + 2 * entries * part),
        4 * rows * entries,
    )


def score_kernel(every, queries, out):
    count = queries.shape[1]
    block = every[...]
    out[:, :count] = jnp.dot(block, queries[...], preferred_element_type=F32)
    block = block.astype(F32)
    square = jnp.sum(block * block, axis=1, keepdims=True)
    out[:, count:] = jnp.broadcast_to(square, (block.shape[0], HEAD))


def score(every, queries):
    passages, part = every.shape
    count = queries.shape[1]
    return call(
        score_kernel,
        (every, queries),
        [VMEM] * 2,
        jax.ShapeDtypeStruct((passages, count + HEAD), F32),
        [],
        2 * passages * part * count,
        2 * part * count + 4 * passages * count,
    )


def finish_kernel(mine, other, squares, similarity, log_norm):
    count = similarity.shape[1]
    total = mine[...] + other[...]
    scale = lax.rsqrt(total[:, count : count + 1] + 1e-06) / logit_divisor
    scores = total[:, :count] * scale * lax.rsqrt(squares[...] + 1e-06)
    similarity[...] = scores
    top = jnp.max(scores, axis=0, keepdims=True)
    log_norm[...] = top + jnp.log(jnp.sum(jnp.exp(scores - top), axis=0, keepdims=True))


def finish(mine, other, squares):
    passages, wide = mine.shape
    count = squares.shape[1]
    return call(
        finish_kernel,
        (mine, other, squares),
        [VMEM] * 3,
        (
            jax.ShapeDtypeStruct((passages, count), F32),
            jax.ShapeDtypeStruct((1, count), F32),
        ),
        [],
        8 * passages * count,
        12 * passages * count,
        passages * count,
    )


def local(
    hidden_in, norm_gain, w_query, w_key, w_value, w_out, final_gain, latents, token_mask, queries
):
    length, part_width = hidden_in.shape[1:]
    dp, tensor = lax.axis_index("dp"), lax.axis_index("tensor")
    y, x_hi, z = dp // 8, (dp // 4) % 2, dp % 4
    x_lo, core = tensor // 2, tensor % 2

    def table(passage):
        return jnp.stack([y, x_hi, z, x_lo, core, jnp.int32(passage)]).astype(jnp.int32)

    def halves(part):
        taken = []
        for weights in (w_query, w_key, w_value):
            wide = weights.shape[1] // 2
            taken.append(lax.dynamic_slice_in_dim(weights, part * wide, wide, 1))
        return jnp.concatenate(taken, axis=1)

    own = hidden_in[0]
    hidden = over_x(own)

    mine = halves(x_hi)
    other = swap_x_hi(halves(1 - x_hi))
    mine_line = jnp.concatenate(direct(mine, first_leg), axis=0)
    other_line = jnp.concatenate(direct(other, first_leg), axis=0)
    w_pieces = ring(mine_line, second_leg) + ring(other_line, second_leg)

    block = move(w_out, lambda y, a, z, b, c: (2 * b + c, a, z, y // 2, y % 2))
    block = behind(block, mine_line)
    out_line = jnp.concatenate(direct(block, first_leg), axis=0)
    out_line = behind(out_line, w_pieces[6], w_pieces[7])
    out_pieces = direct(out_line, second_leg)

    mask_other = swap_x_hi(token_mask)
    masks = (
        jnp.where(x_hi == 0, token_mask, mask_other).astype(F32),
        jnp.where(x_hi == 0, mask_other, token_mask).astype(F32),
    )
    biases = tuple(
        jnp.broadcast_to(jnp.where(mask[0][:, None] > 0, 0.0, -1e30).astype(F32), (length, HEAD))
        for mask in masks
    )
    half = HEAD // 2
    freqs = 10000.0 ** (-2.0 * jnp.arange(half, dtype=F32) / HEAD)
    angle = jnp.arange(length, dtype=F32)[:, None] * freqs[None, :]
    cosine = jnp.concatenate([jnp.cos(angle), jnp.cos(angle)], axis=1)
    sine = jnp.concatenate([-jnp.sin(angle), jnp.sin(angle)], axis=1)

    q_f = queries.astype(F32)
    question_norm_sq = jnp.sum(q_f * q_f, -1)[None]
    question_norm_sq = question_norm_sq + swap_core(question_norm_sq)
    question_norm_sq = question_norm_sq + swap_x_lo(question_norm_sq)
    queries_t = queries.T
    norm_gain, queries_t, question_norm_sq, cosine, sine, biases, masks = lax.optimization_barrier(
        (norm_gain, queries_t, question_norm_sq, cosine, sine, biases, masks)
    )

    pooled = []
    for passage in range(2):
        at = table(passage)
        normed = normalize(at, hidden, norm_gain[None])
        attended = attend(at, normed, w_pieces, cosine, sine, biases[passage])
        gathered = over_x(attended)
        h, square = project(at, gathered, out_pieces, (own, hidden[3], hidden[4]))
        square = square + swap_core(square)
        square = square + swap_x_lo(square)
        square = square + swap_x_hi(square)
        pooled.append(pool(at, h, square, final_gain[None], latents, masks[passage]))

    emb = jnp.concatenate(pooled, axis=0).astype(BF16)
    emb_other = swap_x_hi(emb)
    emb = jnp.concatenate(
        [jnp.where(x_hi == 0, emb, emb_other), jnp.where(x_hi == 0, emb_other, emb)], axis=1
    )

    def gather4(values, axis, position):
        def where(step):
            def to(y, a, z, b, c):
                if axis == 0:
                    return ((y + step) % 4, a, z, b, c)
                return (y, a, (z + step) % 4, b, c)

            return to

        parts = [values] + [move(values, where(step)) for step in (1, 2, 3)]
        out = jnp.zeros(values.shape[:axis] + (4,) + values.shape[axis + 1 :], values.dtype)
        for step, piece in enumerate(parts):
            at = [0] * values.ndim
            at[axis] = (position - step) % 4
            out = lax.dynamic_update_slice(out, piece, at)
        return out

    emb = emb[None, :, None]
    emb = gather4(gather4(emb, 2, z), 0, y)
    products = score(emb.reshape(32, part_width), queries_t)
    products = products + swap_core(products)
    similarity, log_norm = finish(products, swap_x_lo(products), question_norm_sq)
    return (similarity.T, log_norm[0])


def solution(mesh):
    placed = (
        P("dp", None, "tensor"),
        P(),
        P("dp", "tensor"),
        P("dp", "tensor"),
        P("dp", "tensor"),
        P("tensor", "dp"),
        P("tensor"),
        P(None, "tensor"),
        P("dp", None),
        P("dp", "tensor"),
    )
    return jax.shard_map(
        local, mesh=mesh, in_specs=placed, out_specs=(P("dp", None), P("dp")), check_vma=False
    )
```

```python
import jax
import jax.numpy as jnp
from jax import lax
from jax.experimental import pallas as pl
from jax.experimental.pallas import tpu as pltpu
from jax.sharding import PartitionSpec as P

HEAD = 128
EPS = 1e-05
logit_divisor = 0.02
BOTH = ("dp", "tensor")
COORDS = [
    (y, a, z, b, c)
    for y in range(4)
    for a in range(2)
    for z in range(4)
    for b in range(2)
    for c in range(2)
]


def index_of(y, a, z, b, c):
    return (((y * 2 + a) * 4 + z) * 2 + b) * 2 + c


def move(values, where, when=lambda *at: True):
    pairs = [(index_of(*at), index_of(*where(*at))) for at in COORDS if when(*at)]
    return lax.ppermute(values, BOTH, pairs)


def swap_core(values):
    return move(values, lambda y, a, z, b, c: (y, a, z, b, 1 - c))


def swap_x_hi(values):
    return move(values, lambda y, a, z, b, c: (y, 1 - a, z, b, c))


def swap_x_lo(values):
    return move(values, lambda y, a, z, b, c: (y, a, z, 1 - b, c))


def swap_x_next(values):
    return move(values, lambda y, a, z, b, c: (y, 1 - a, z, 1 - b, c))


def along_x(step):
    def where(y, a, z, b, c):
        x = (2 * a + b + step) % 4
        return (y, x // 2, z, x % 2, c)

    return where


def first_leg(step):
    def where(y, a, z, b, c):
        if c == 0:
            return ((y + step) % 4, a, z, b, c)
        return (y, a, (z + step) % 4, b, c)

    return where


def second_leg(step):
    def where(y, a, z, b, c):
        if c == 0:
            return (y, a, (z + step) % 4, b, c)
        return ((y + step) % 4, a, z, b, c)

    return where


def ring(values, leg):
    half = values.shape[0] // 2
    before = move(values, leg(1))
    after = move(values, leg(-1))
    far_low = move(before[:half], leg(1))
    far_high = move(after[half:], leg(-1))
    return values, before, after, far_low, far_high


def direct(values, leg):
    return values, move(values, leg(1)), move(values, leg(-1)), move(values, leg(2))


def passages_over_x(own):
    def holds(step):
        def when(y, a, z, b, c):
            return (2 * a + b + step) % 4 // 2 == c

        return when

    rows = own.shape[0]
    other = move(own, lambda y, a, z, b, c: (y, a, z, b, a), lambda y, a, z, b, c: c != a)
    whole = jnp.concatenate([own, other], axis=0)
    before = move(whole, along_x(1), holds(0))
    after = move(whole, along_x(-1), holds(0))
    far_low = move(before[:rows], along_x(1), holds(-1))
    far_high = move(after[rows:], along_x(-1), holds(1))
    return whole, before, after, far_low, far_high


def behind(values, *others):
    return lax.optimization_barrier((values,) + others)[0]


AT_Y, AT_X_HI, AT_Z, AT_X_LO, AT_CORE = range(5)
VMEM = pl.BlockSpec(memory_space=pltpu.VMEM)
SMEM = pl.BlockSpec(memory_space=pltpu.SMEM)
ANY = pl.BlockSpec(memory_space=pl.ANY)
F32, BF16 = jnp.float32, jnp.bfloat16
OFFSETS = (0, 3, 1, 2)
NT = (((1,), (1,)), ((), ()))
RATE = 1.15e9
EXPONENT = HEAD ** (-0.5) * 1.4426950408889634


def call(kernel, args, specs, out, scratch, micros, mib=48):
    return pl.pallas_call(
        kernel,
        out_shape=out,
        in_specs=specs,
        out_specs=jax.tree.map(lambda _: VMEM, out),
        scratch_shapes=scratch,
        compiler_params=pltpu.CompilerParams(vmem_limit_bytes=mib * 1024 * 1024),
        cost_estimate=pl.CostEstimate(
            flops=int(micros * RATE), bytes_accessed=1024, transcendentals=0
        ),
    )(*args)


def leg_positions(at, core, first, second):
    y = jnp.where(core == 0, at[AT_Y] + first, at[AT_Y] + second) % 4
    z = jnp.where(core == 0, at[AT_Z] + second, at[AT_Z] + first) % 4
    return y, z


def project_kernel(at, *refs):
    whole, before, after, low, high, gain = refs[:6]
    lines, others = refs[6:9], refs[9:12]
    total, far, far_other, tokens, weights, weights_other, sems, w_sems = refs[12:]
    rows, part = low.shape
    a, b, core = at[AT_X_HI], at[AT_X_LO], at[AT_CORE]
    here = a == core
    near = jnp.logical_or(
        jnp.logical_and(here, b == 0), jnp.logical_and(jnp.logical_not(here), b == 1)
    )

    def send(src, block, sem):
        column = pl.multiple_of(block * part, part)
        return pltpu.make_async_copy(src, tokens.at[:, pl.ds(column, part)], sems.at[sem])

    first, second = 2 * b + core, 2 * b + 1 - core
    third, fourth = 2 * (1 - b) + core, 2 * (1 - b) + 1 - core

    @pl.when(here)
    def _():
        send(whole.at[pl.ds(0, rows)], first, 0).start()
        send(whole.at[pl.ds(rows, rows)], second, 1).start()

    @pl.when(jnp.logical_not(here))
    def _():
        send(low, first, 0).start()
        send(high, second, 1).start()

    @pl.when(near)
    def _():
        send(after.at[pl.ds(0, rows)], third, 2).start()
        send(after.at[pl.ds(rows, rows)], fourth, 3).start()

    @pl.when(jnp.logical_not(near))
    def _():
        send(before.at[pl.ds(0, rows)], third, 2).start()
        send(before.at[pl.ds(rows, rows)], fourth, 3).start()

    deep, wide = lines[0].shape
    copies = []
    for k in range(3):
        for source, target in ((lines[k], weights), (others[k], weights_other)):
            copies.append(
                pltpu.make_async_copy(
                    source, target.at[pl.ds(k * deep, deep)], w_sems.at[len(copies)]
                )
            )
    for copy in copies:
        copy.start()
    for sem in range(4):
        send(low, 0, sem).wait()

    width = tokens.shape[1]
    tile = 64

    @pl.loop(0, rows // tile)
    def _(step):
        at_rows = pl.ds(pl.multiple_of(step * tile, tile), tile)
        squares = jnp.zeros((tile, HEAD), F32)
        for lane in range(0, width, HEAD):
            block = tokens[at_rows, lane : lane + HEAD].astype(F32)
            squares = squares + block * block
        mean = jnp.sum(squares, axis=-1, keepdims=True) / width
        scale = jnp.broadcast_to(lax.rsqrt(mean + EPS), (tile, HEAD))
        for lane in range(0, width, HEAD):
            block = tokens[at_rows, lane : lane + HEAD].astype(F32)
            own_gain = gain[:, lane : lane + HEAD].astype(F32)
            tokens[at_rows, lane : lane + HEAD] = (block * scale * own_gain).astype(BF16)

    entry_rows = deep // 8

    def chunk(leg_core, second):
        taken = []
        for first in OFFSETS:
            y, z = leg_positions(at, leg_core, first, second)
            for entry in range(2):
                row = (y * 8 + (a + entry) % 2 * 4 + z) * entry_rows
                taken.append(tokens[:, pl.ds(pl.multiple_of(row, entry_rows), entry_rows)])
        return jnp.concatenate(taken, axis=1)

    far[...] = chunk(core, OFFSETS[3])
    far_other[...] = chunk(1 - core, OFFSETS[3])
    for two in range(3):
        for k, (leg_core, held) in enumerate(((core, weights), (1 - core, weights_other))):
            copies[2 * two + k].wait()
            product = jnp.dot(
                chunk(leg_core, OFFSETS[two]),
                held[two * deep : (two + 1) * deep, :],
                preferred_element_type=F32,
            )
            cols = slice(k * wide, (k + 1) * wide)
            total[:, cols] = product if two == 0 else total[:, cols] + product


def project_part(at, hidden, gain, lines, others):
    rows, width = hidden[3].shape[0], gain.shape[1]
    deep, wide = lines[0].shape
    return call(
        project_kernel,
        (at, *hidden, gain, *lines, *others),
        [SMEM] + [ANY] * 5 + [VMEM] + [ANY] * 6,
        (
            jax.ShapeDtypeStruct((rows, 2 * wide), F32),
            jax.ShapeDtypeStruct((rows, deep), BF16),
            jax.ShapeDtypeStruct((rows, deep), BF16),
        ),
        [
            pltpu.VMEM((rows, width), BF16),
            pltpu.VMEM((3 * deep, wide), BF16),
            pltpu.VMEM((3 * deep, wide), BF16),
            pltpu.SemaphoreType.DMA((4,)),
            pltpu.SemaphoreType.DMA((6,)),
        ],
        10.0,
    )


def attention_kernel(partial, far, far_other, *refs):
    pieces, (cosine, sine, bias, out, total, qkv) = refs[:4], refs[4:]
    rows, half = partial.shape[0], pieces[0].shape[0]
    wide = partial.shape[1] // 2
    heads = wide // HEAD - 2
    for k, taken in enumerate((far, far_other)):
        base = k * wide
        low, high = pieces[2 * k], pieces[2 * k + 1]
        total[...] = (
            partial[:, base : base + wide]
            + jnp.dot(taken[:, :half], low[...], preferred_element_type=F32)
            + jnp.dot(taken[:, half:], high[...], preferred_element_type=F32)
        )
        for head in range(heads + 1):
            cols = slice(head * HEAD, (head + 1) * HEAD)
            block = total[:, cols]
            turned = block * cosine[...] + pltpu.roll(block, HEAD // 2, 1) * sine[...]
            qkv[:, cols] = turned.astype(BF16)
        keys = qkv[:, heads * HEAD : (heads + 1) * HEAD]
        values_t = total[:, (heads + 1) * HEAD :].T.astype(BF16)
        for head in range(heads):
            query = qkv[:, head * HEAD : (head + 1) * HEAD]
            logits = lax.dot_general(keys, query, NT, preferred_element_type=F32)
            logits = logits + jnp.concatenate([bias[...]] * (rows // HEAD), axis=1)
            top = jnp.max(logits, axis=0, keepdims=True)
            power = jnp.exp2((logits - top) * EXPONENT)
            share = 1.0 / jnp.sum(power, axis=0, keepdims=True)
            mixed = jnp.dot(values_t, power.astype(BF16), preferred_element_type=F32)
            start = (k * heads + head) * HEAD
            out[:, start : start + HEAD] = (mixed * share).T.astype(BF16)


def attend(parts, pieces, cosine, sine, bias):
    rows, wide = parts[0].shape
    heads = wide // HEAD - 4
    return call(
        attention_kernel,
        (*parts, *pieces, cosine, sine, bias),
        [VMEM] * 10,
        jax.ShapeDtypeStruct((rows, heads * HEAD), BF16),
        [pltpu.VMEM((rows, wide // 2), F32), pltpu.VMEM((rows, wide // 2), BF16)],
        8.0,
    )


def output_kernel(at, *refs):
    attended, blocks, others = refs[:3], refs[3:7], refs[7:11]
    whole, low, high = refs[11:14]
    partial, w_far, weights, residual, sems, r_sems = refs[14:]
    rows, wide = attended[0].shape
    part = wide // 2
    count = weights.shape[0] // 4
    a, b, core = at[AT_X_HI], at[AT_X_LO], at[AT_CORE]
    copies = []
    for two, second in enumerate(OFFSETS):
        for one, first in enumerate(OFFSETS):
            for k, (held, leg_core) in enumerate(((blocks, core), (others, 1 - core))):
                y, z = leg_positions(at, leg_core, first, second)
                column = pl.multiple_of(k * part + z * HEAD, HEAD)
                copies.append(
                    pltpu.make_async_copy(
                        held[two].at[pl.ds(one * count, count)],
                        weights.at[
                            pl.ds(pl.multiple_of(y * count, count), count), pl.ds(column, HEAD)
                        ],
                        sems.at[len(copies)],
                    )
                )
    for copy in copies:
        copy.start()
    columns = pl.ds(pl.multiple_of(a * part, part), part)

    def keep(src, k):
        return pltpu.make_async_copy(
            src.at[:, columns], residual.at[:, pl.ds(k * part, part)], r_sems.at[k]
        )

    @pl.when(a == core)
    def _():
        keep(whole.at[pl.ds(0, rows)], 0).start()
        keep(whole.at[pl.ds(rows, rows)], 1).start()

    @pl.when(a != core)
    def _():
        keep(low, 0).start()
        keep(high, 1).start()

    keep(low, 0).wait()
    keep(high, 1).wait()
    for copy in copies:
        copy.wait()

    def held_rows(offset, k):
        chip = (2 * a + b + offset) % 4
        there = core if k == 0 else 1 - core
        row = ((chip % 2 * 2 + there) * 2 + chip // 2) * part
        return weights[pl.ds(pl.multiple_of(row, part), part), :]

    for k in range(2):
        w_far[k * part : (k + 1) * part, :] = held_rows(2, k)
    partial[...] = residual[...].astype(F32)
    for piece, offset in zip(attended, OFFSETS[:3], strict=True):
        for k in range(2):
            partial[...] += jnp.dot(
                piece[:, k * part : (k + 1) * part],
                held_rows(offset, k),
                preferred_element_type=F32,
            )


def output_part(at, attended, blocks, others, hidden):
    rows, wide = attended[0].shape
    width = blocks[0].shape[0]
    return call(
        output_kernel,
        (at, *attended, *blocks, *others, *hidden),
        [SMEM] + [VMEM] * 3 + [ANY] * 11,
        (jax.ShapeDtypeStruct((rows, wide), F32), jax.ShapeDtypeStruct((wide, wide), BF16)),
        [
            pltpu.VMEM((width, wide), BF16),
            pltpu.VMEM((rows, wide), BF16),
            pltpu.SemaphoreType.DMA((32,)),
            pltpu.SemaphoreType.DMA((2,)),
        ],
        7.0,
    )


def output_rest_kernel(partial, low, high, w_far, h, square):
    half, wide = low.shape
    for k, piece in enumerate((low, high)):
        at_rows = slice(k * half, (k + 1) * half)
        product = jnp.dot(piece[...], w_far[...], preferred_element_type=F32)
        block = (partial[at_rows, :] + product).astype(BF16)
        h[at_rows, :] = block
        block = block.astype(F32)
        block = block * block
        folded = block[:, :HEAD]
        for lane in range(HEAD, wide, HEAD):
            folded = folded + block[:, lane : lane + HEAD]
        square[:, at_rows] = jnp.sum(folded.T, axis=0, keepdims=True)


def output_rest(partial, w_far, low, high):
    rows, wide = partial.shape
    return call(
        output_rest_kernel,
        (partial, low, high, w_far),
        [VMEM] * 4,
        (jax.ShapeDtypeStruct((rows, wide), BF16), jax.ShapeDtypeStruct((1, rows), F32)),
        [],
        3.0,
        mib=24,
    )


def pool_kernel(width, h, square, packed, packed_other, mask, out):
    rows, wide = h.shape
    entries = packed.shape[0] - 16
    scale = jnp.broadcast_to(lax.rsqrt(square[...] / width + EPS), (HEAD, rows)).T
    keep = jnp.broadcast_to(mask[...], (HEAD, rows)).T
    count = jnp.sum(mask[...], axis=1, keepdims=True)
    heads = wide // HEAD
    for head in range(heads):
        cols = slice(head * HEAD, (head + 1) * HEAD)
        held = packed if head < heads // 2 else packed_other
        start = head % (heads // 2) * HEAD
        gain = held[entries : entries + 1, start : start + HEAD].astype(F32)
        block = (h[:, cols].astype(F32) * scale * gain).astype(BF16)
        lat = held[:entries, start : start + HEAD]
        logits = lax.dot_general(lat, block, NT, preferred_element_type=F32)
        top = jnp.max(logits, axis=0, keepdims=True)
        power = jnp.exp2((logits - top) * EXPONENT)
        share = mask[...] / jnp.sum(power, axis=0, keepdims=True)
        power = power * share
        folded = power[:, :HEAD]
        for k in range(1, rows // HEAD):
            folded = folded + power[:, k * HEAD : (k + 1) * HEAD]
        taken = jnp.sum(folded, axis=1, keepdims=True)
        cross = jnp.sum(taken * lat.astype(F32), axis=0, keepdims=True)
        kept = jnp.sum(block.astype(F32) * keep, axis=0, keepdims=True)
        out[:, cols] = (cross + kept) / count


def pool(h, square, packed, packed_other, mask):
    rows, wide = h.shape

    def kernel(*refs):
        pool_kernel(4 * wide, *refs)

    return call(
        kernel,
        (h, square, packed, packed_other, mask),
        [VMEM] * 5,
        jax.ShapeDtypeStruct((1, wide), F32),
        [],
        5.0,
        mib=24,
    )


def score_kernel(every, queries, out):
    count = queries.shape[1]
    block = every[...]
    out[:, :count] = jnp.dot(block, queries[...], preferred_element_type=F32)
    block = block.astype(F32)
    square = jnp.sum(block * block, axis=1, keepdims=True)
    out[:, count:] = jnp.broadcast_to(square, (block.shape[0], HEAD))


def score(every, queries):
    passages, part = every.shape
    count = queries.shape[1]
    return call(
        score_kernel,
        (every, queries),
        [VMEM] * 2,
        jax.ShapeDtypeStruct((passages, count + HEAD), F32),
        [],
        0.8,
        mib=24,
    )


def finish_kernel(mine, other, squares, similarity, log_norm):
    count = similarity.shape[1]
    total = mine[...] + other[...]
    scale = lax.rsqrt(total[:, count : count + 1] + 1e-06) / logit_divisor
    scores = total[:, :count] * scale * lax.rsqrt(squares[...] + 1e-06)
    similarity[...] = scores
    top = jnp.max(scores, axis=0, keepdims=True)
    log_norm[...] = top + jnp.log(jnp.sum(jnp.exp(scores - top), axis=0, keepdims=True))


def finish(mine, other, squares):
    passages, wide = mine.shape
    count = squares.shape[1]
    return call(
        finish_kernel,
        (mine, other, squares),
        [VMEM] * 3,
        (
            jax.ShapeDtypeStruct((passages, count), F32),
            jax.ShapeDtypeStruct((1, count), F32),
        ),
        [],
        0.8,
        mib=24,
    )


def local(
    hidden_in, norm_gain, w_query, w_key, w_value, w_out, final_gain, latents, token_mask, queries
):
    length, part_width = hidden_in.shape[1:]
    part = part_width // 2
    dp, tensor = lax.axis_index("dp"), lax.axis_index("tensor")
    y, x_hi, z = dp // 8, (dp // 4) % 2, dp % 4
    x_lo, core = tensor // 2, tensor % 2
    at = jnp.stack([y, x_hi, z, x_lo, core]).astype(jnp.int32)

    def halves(side):
        taken = []
        for weights in (w_query, w_key, w_value):
            wide = weights.shape[1] // 2
            taken.append(lax.dynamic_slice_in_dim(weights, side * wide, wide, 1))
        return jnp.concatenate(taken, axis=1)

    hidden = passages_over_x(hidden_in[0])
    mask_other = swap_x_hi(token_mask)

    half = HEAD // 2
    freqs = 10000.0 ** (-2.0 * jnp.arange(half, dtype=F32) / HEAD)
    angle = jnp.arange(length, dtype=F32)[:, None] * freqs[None, :]
    cosine = jnp.concatenate([jnp.cos(angle), jnp.cos(angle)], axis=1)
    sine = jnp.concatenate([-jnp.sin(angle), jnp.sin(angle)], axis=1)

    shard = jnp.concatenate([halves(x_hi), swap_x_hi(halves(1 - x_hi))], axis=0)
    shard, cosine, sine, mask_other, _ = lax.optimization_barrier(
        (shard, cosine, sine, mask_other, hidden[0])
    )
    line = jnp.concatenate(direct(shard, first_leg), axis=0)
    w_pieces = ring(line, second_leg)
    w_others = tuple(swap_core(piece) for piece in w_pieces)

    block = behind(w_out, hidden[3], hidden[4])
    block = move(block, lambda y, a, z, b, c: (2 * b + c, a, z, y // 2, y % 2))
    out_line = jnp.concatenate(direct(block, first_leg), axis=0)
    out_pieces = direct(out_line, second_leg)
    out_others = tuple(swap_core(piece) for piece in out_pieces)

    mask = jnp.where(x_hi == core, token_mask, mask_other)
    bias = jnp.where(mask[0][:, None] > 0, 0.0, -1e30).astype(F32)
    bias = jnp.broadcast_to(bias, (length, HEAD))
    mask = mask.astype(F32)
    lat = lax.dynamic_slice_in_dim(behind(latents, hidden[3], hidden[4]), x_hi * part, part, 1)
    gain = lax.dynamic_slice_in_dim(final_gain, x_hi * part, part, 0)
    packed = jnp.concatenate([lat, jnp.broadcast_to(gain[None], (16, part))], axis=0)
    packed_other = swap_core(packed)

    parts = project_part(at, hidden, norm_gain[None], w_pieces[:3], w_others[:3])
    attended = attend(parts, w_pieces[3:] + w_others[3:], cosine, sine, bias)
    gathered = ring(attended, along_x)

    queries_then = behind(queries, attended)
    q_f = queries_then.astype(F32)
    question_norm_sq = jnp.sum(q_f * q_f, -1)[None]
    queries_t = queries_then.T
    question_norm_sq = question_norm_sq + swap_core(question_norm_sq)
    question_norm_sq = question_norm_sq + swap_x_lo(question_norm_sq)

    partial, w_far = output_part(
        at, gathered[:3], out_pieces, out_others, (hidden[0], hidden[3], hidden[4])
    )
    partial, question_norm_sq, queries_t, packed_other = lax.optimization_barrier(
        (partial, question_norm_sq, queries_t, packed_other)
    )
    h, square = output_rest(partial, w_far, gathered[3], gathered[4])
    square = square + swap_x_lo(square)
    square = square + swap_x_next(square)
    pooled = pool(h, square, packed, packed_other, mask)

    def in_order(first, values, other, axis):
        low, high = jnp.where(first, values, other), jnp.where(first, other, values)
        return jnp.concatenate([low, high], axis=axis)

    emb = pooled.astype(BF16)
    emb = in_order(core == 0, emb[:, :part], swap_core(emb[:, part:]), 0)
    emb = in_order(x_hi == 0, emb, swap_x_hi(emb), 1)
    emb = emb[None, :, None]
    emb = in_order(z % 2 == 0, emb, move(emb, lambda y, a, z, b, c: (y, a, z ^ 1, b, c)), 2)
    emb = in_order(z < 2, emb, move(emb, lambda y, a, z, b, c: (y, a, 3 - z, b, c)), 2)
    emb = in_order(y % 2 == 0, emb, move(emb, lambda y, a, z, b, c: (y ^ 1, a, z, b, c)), 0)
    emb = in_order(y < 2, emb, move(emb, lambda y, a, z, b, c: (3 - y, a, z, b, c)), 0)
    products = score(emb.reshape(32, part_width), queries_t)
    products = products + swap_core(products)
    similarity, log_norm = finish(products, swap_x_lo(products), question_norm_sq)
    return (similarity.T, log_norm[0])


def solution(mesh):
    placed = (
        P("dp", None, "tensor"),
        P(),
        P("dp", "tensor"),
        P("dp", "tensor"),
        P("dp", "tensor"),
        P("tensor", "dp"),
        P("tensor"),
        P(None, "tensor"),
        P("dp", None),
        P("dp", "tensor"),
    )
    return jax.shard_map(
        local, mesh=mesh, in_specs=placed, out_specs=(P("dp", None), P("dp")), check_vma=False
    )
```

```python
import jax
import jax.numpy as jnp
from jax import lax
from jax.experimental import pallas as pl
from jax.experimental.pallas import tpu as pltpu
from jax.sharding import PartitionSpec as P

HEAD = 128
EPS = 1e-05
logit_divisor = 0.02
BOTH = ("dp", "tensor")
COORDS = [
    (y, a, z, b, c)
    for y in range(4)
    for a in range(2)
    for z in range(4)
    for b in range(2)
    for c in range(2)
]


def index_of(y, a, z, b, c):
    return (((y * 2 + a) * 4 + z) * 2 + b) * 2 + c


def move(values, where, when=lambda *at: True):
    pairs = [(index_of(*at), index_of(*where(*at))) for at in COORDS if when(*at)]
    return lax.ppermute(values, BOTH, pairs)


def swap_core(values):
    return move(values, lambda y, a, z, b, c: (y, a, z, b, 1 - c))


def swap_x_hi(values):
    return move(values, lambda y, a, z, b, c: (y, 1 - a, z, b, c))


def swap_x_lo(values):
    return move(values, lambda y, a, z, b, c: (y, a, z, 1 - b, c))


def swap_x_next(values):
    return move(values, lambda y, a, z, b, c: (y, 1 - a, z, 1 - b, c))


def along_x(step):
    def where(y, a, z, b, c):
        x = (2 * a + b + step) % 4
        return (y, x // 2, z, x % 2, c)

    return where


def first_leg(step):
    def where(y, a, z, b, c):
        if c == 0:
            return ((y + step) % 4, a, z, b, c)
        return (y, a, (z + step) % 4, b, c)

    return where


def second_leg(step):
    def where(y, a, z, b, c):
        if c == 0:
            return (y, a, (z + step) % 4, b, c)
        return ((y + step) % 4, a, z, b, c)

    return where


def near(values, leg):
    return move(values, leg(1)), move(values, leg(-1))


def halves_of(before, after):
    half = before.shape[0] // 2
    return before[:half], after[half:]


def far(low, high, leg):
    return move(low, leg(1)), move(high, leg(-1))


def direct(values, leg):
    return values, move(values, leg(1)), move(values, leg(-1)), move(values, leg(2))


def holds(step):
    def when(y, a, z, b, c):
        return (2 * a + b + step) % 4 // 2 == c

    return when


def behind(values, *others):
    return lax.optimization_barrier((values,) + others)[0]


AT_Y, AT_X_HI, AT_Z, AT_X_LO, AT_CORE = range(5)
VMEM = pl.BlockSpec(memory_space=pltpu.VMEM)
SMEM = pl.BlockSpec(memory_space=pltpu.SMEM)
HBM = pl.BlockSpec(memory_space=pltpu.HBM)
F32, BF16 = jnp.float32, jnp.bfloat16
OFFSETS = (0, 3, 1, 2)
NT = (((1,), (1,)), ((), ()))
RATE = 1.15e9
EXPONENT = HEAD ** (-0.5) * 1.4426950408889634


def call(kernel, args, specs, out, scratch, micros, mib=48):
    return pl.pallas_call(
        kernel,
        out_shape=out,
        in_specs=specs,
        out_specs=jax.tree.map(lambda _: VMEM, out),
        scratch_shapes=scratch,
        compiler_params=pltpu.CompilerParams(vmem_limit_bytes=mib * 1024 * 1024),
        cost_estimate=pl.CostEstimate(
            flops=int(micros * RATE), bytes_accessed=1024, transcendentals=0
        ),
    )(*args)


def leg_positions(at, core, first, second):
    y = jnp.where(core == 0, at[AT_Y] + first, at[AT_Y] + second) % 4
    z = jnp.where(core == 0, at[AT_Z] + second, at[AT_Z] + first) % 4
    return y, z


def norm_kernel(at, *refs):
    whole, before, after, low, high, gain, own, other, residual, tokens, sems = refs
    rows, part = low.shape
    a, b, core = at[AT_X_HI], at[AT_X_LO], at[AT_CORE]
    here = a == core
    near = jnp.logical_or(
        jnp.logical_and(here, b == 0), jnp.logical_and(jnp.logical_not(here), b == 1)
    )

    def send(src, block, sem):
        column = pl.multiple_of(block * part, part)
        return pltpu.make_async_copy(src, tokens.at[:, pl.ds(column, part)], sems.at[sem])

    first, second = 2 * b + core, 2 * b + 1 - core
    third, fourth = 2 * (1 - b) + core, 2 * (1 - b) + 1 - core

    @pl.when(here)
    def _():
        send(whole.at[pl.ds(0, rows)], first, 0).start()
        send(whole.at[pl.ds(rows, rows)], second, 1).start()

    @pl.when(jnp.logical_not(here))
    def _():
        send(low, first, 0).start()
        send(high, second, 1).start()

    @pl.when(near)
    def _():
        send(after.at[pl.ds(0, rows)], third, 2).start()
        send(after.at[pl.ds(rows, rows)], fourth, 3).start()

    @pl.when(jnp.logical_not(near))
    def _():
        send(before.at[pl.ds(0, rows)], third, 2).start()
        send(before.at[pl.ds(rows, rows)], fourth, 3).start()

    for sem in range(4):
        send(low, 0, sem).wait()

    own_columns = part // 2
    for k, held in enumerate((first, second)):
        lane = pl.multiple_of(held * part + a * own_columns, own_columns)
        residual[:, k * own_columns : (k + 1) * own_columns] = tokens[:, pl.ds(lane, own_columns)]

    width = tokens.shape[1]
    tile = 64
    lanes = []
    for two, later in enumerate(OFFSETS):
        for one, sooner in enumerate(OFFSETS):
            y, z = leg_positions(at, core, sooner, later)
            for entry in range(2):
                lane = pl.multiple_of((y * 8 + (a + entry) % 2 * 4 + z) * HEAD, HEAD)
                mine = ((two * 4 + one) * 2 + entry) * HEAD
                turned = ((one * 4 + two) * 2 + entry) * HEAD
                lanes.append((pl.ds(lane, HEAD), mine, turned))

    @pl.loop(0, rows // tile)
    def _(step):
        at_rows = pl.ds(pl.multiple_of(step * tile, tile), tile)
        squares = jnp.zeros((tile, HEAD), F32)
        for lane in range(0, width, HEAD):
            values = tokens[at_rows, lane : lane + HEAD].astype(F32)
            squares = squares + values * values
        mean = jnp.sum(squares, axis=-1, keepdims=True) / width
        scale = jnp.broadcast_to(lax.rsqrt(mean + EPS), (tile, HEAD))
        for lane, mine, turned in lanes:
            values = tokens[at_rows, lane].astype(F32) * scale * gain[:, lane]
            values = values.astype(BF16)
            own[at_rows, mine : mine + HEAD] = values
            other[at_rows, turned : turned + HEAD] = values


def normalize(at, hidden, gain):
    rows, part = hidden[3].shape
    width = gain.shape[1]
    return call(
        norm_kernel,
        (at, *hidden, gain),
        [SMEM] + [HBM] * 5 + [VMEM],
        (
            jax.ShapeDtypeStruct((rows, width), BF16),
            jax.ShapeDtypeStruct((rows, width), BF16),
            jax.ShapeDtypeStruct((rows, part), BF16),
        ),
        [pltpu.VMEM((rows, width), BF16), pltpu.SemaphoreType.DMA((4,))],
        30.0,
        mib=16,
    )


def project_kernel(own, other, *refs):
    lines, total, done = refs[:6], refs[6], refs[7]
    done[...] = jnp.zeros_like(done)
    deep, wide = lines[0].shape
    for k, normed in enumerate((own, other)):
        total[:, k * wide : (k + 1) * wide] = sum(
            jnp.dot(
                normed[:, j * deep : (j + 1) * deep],
                lines[3 * k + j][...],
                preferred_element_type=F32,
            )
            for j in range(3)
        )


def project_part(own, other, lines, others):
    rows = own.shape[0]
    wide = lines[0].shape[1]
    return call(
        project_kernel,
        (own, other, *lines, *others),
        [VMEM] * 8,
        (jax.ShapeDtypeStruct((rows, 2 * wide), F32), jax.ShapeDtypeStruct((8, HEAD), F32)),
        [],
        7.0,
        mib=20,
    )


def attention_kernel(partial, own, other, *refs):
    pieces, (cosine, sine, bias, out, done, total, qkv) = refs[:4], refs[4:]
    done[...] = jnp.zeros_like(done)
    rows = partial.shape[0]
    half = pieces[0].shape[0]
    wide = partial.shape[1] // 2
    heads = wide // HEAD - 2
    for k, normed in enumerate((own, other)):
        base = k * wide
        start = normed.shape[1] - 2 * half
        total[...] = (
            partial[:, base : base + wide]
            + jnp.dot(
                normed[:, start : start + half], pieces[2 * k][...], preferred_element_type=F32
            )
            + jnp.dot(
                normed[:, start + half :], pieces[2 * k + 1][...], preferred_element_type=F32
            )
        )
        for head in range(heads + 1):
            cols = slice(head * HEAD, (head + 1) * HEAD)
            block = total[:, cols]
            turned = block * cosine[...] + pltpu.roll(block, HEAD // 2, 1) * sine[...]
            qkv[:, cols] = turned.astype(BF16)
        keys = qkv[:, heads * HEAD : (heads + 1) * HEAD]
        values_t = total[:, (heads + 1) * HEAD :].T.astype(BF16)
        for head in range(heads):
            query = qkv[:, head * HEAD : (head + 1) * HEAD]
            logits = lax.dot_general(keys, query, NT, preferred_element_type=F32)
            logits = logits + jnp.concatenate([bias[...]] * (rows // HEAD), axis=1)
            top = jnp.max(logits, axis=0, keepdims=True)
            power = jnp.exp2((logits - top) * EXPONENT)
            share = 1.0 / jnp.sum(power, axis=0, keepdims=True)
            mixed = jnp.dot(values_t, power.astype(BF16), preferred_element_type=F32)
            start = (k * heads + head) * HEAD
            out[:, start : start + HEAD] = (mixed * share).T.astype(BF16)


def attend(partial, own, other, pieces, cosine, sine, bias):
    rows, wide = partial.shape
    heads = wide // HEAD - 4
    return call(
        attention_kernel,
        (partial, own, other, *pieces, cosine, sine, bias),
        [VMEM] * 10,
        (jax.ShapeDtypeStruct((rows, heads * HEAD), BF16), jax.ShapeDtypeStruct((8, HEAD), F32)),
        [pltpu.VMEM((rows, wide // 2), F32), pltpu.VMEM((rows, wide // 2), BF16)],
        8.0,
        mib=20,
    )


def output_kernel(at, *refs):
    attended, blocks, others = refs[:3], refs[3:7], refs[7:11]
    residual, partial, w_far, weights, sems = refs[11:]
    rows, wide = attended[0].shape
    part = wide // 2
    count = weights.shape[0] // 4
    a, b, core = at[AT_X_HI], at[AT_X_LO], at[AT_CORE]
    copies = []
    for two, second in enumerate(OFFSETS):
        for one, first in enumerate(OFFSETS):
            for k, (held, leg_core) in enumerate(((blocks, core), (others, 1 - core))):
                y, z = leg_positions(at, leg_core, first, second)
                column = pl.multiple_of(k * part + z * HEAD, HEAD)
                copies.append(
                    pltpu.make_async_copy(
                        held[two].at[pl.ds(one * count, count)],
                        weights.at[
                            pl.ds(pl.multiple_of(y * count, count), count), pl.ds(column, HEAD)
                        ],
                        sems.at[len(copies)],
                    )
                )
    for copy in copies:
        copy.start()
    for copy in copies:
        copy.wait()

    def held_rows(offset, k):
        chip = (2 * a + b + offset) % 4
        there = core if k == 0 else 1 - core
        row = ((chip % 2 * 2 + there) * 2 + chip // 2) * part
        return weights[pl.ds(pl.multiple_of(row, part), part), :]

    for k in range(2):
        w_far[k * part : (k + 1) * part, :] = held_rows(2, k)
    partial[...] = residual[...].astype(F32)
    for piece, offset in zip(attended, OFFSETS[:3], strict=True):
        for k in range(2):
            partial[...] += jnp.dot(
                piece[:, k * part : (k + 1) * part],
                held_rows(offset, k),
                preferred_element_type=F32,
            )


def output_part(at, attended, blocks, others, residual):
    rows, wide = attended[0].shape
    width = blocks[0].shape[0]
    return call(
        output_kernel,
        (at, *attended, *blocks, *others, residual),
        [SMEM] + [VMEM] * 3 + [HBM] * 8 + [VMEM],
        (jax.ShapeDtypeStruct((rows, wide), F32), jax.ShapeDtypeStruct((wide, wide), BF16)),
        [
            pltpu.VMEM((width, wide), BF16),
            pltpu.SemaphoreType.DMA((32,)),
        ],
        9.5,
        mib=28,
    )


def output_rest_kernel(partial, low, high, w_far, h, square):
    half, wide = low.shape
    for k, piece in enumerate((low, high)):
        at_rows = slice(k * half, (k + 1) * half)
        product = jnp.dot(piece[...], w_far[...], preferred_element_type=F32)
        block = (partial[at_rows, :] + product).astype(BF16)
        h[at_rows, :] = block
        block = block.astype(F32)
        block = block * block
        folded = block[:, :HEAD]
        for lane in range(HEAD, wide, HEAD):
            folded = folded + block[:, lane : lane + HEAD]
        square[:, at_rows] = jnp.sum(folded.T, axis=0, keepdims=True)


def output_rest(partial, w_far, low, high):
    rows, wide = partial.shape
    return call(
        output_rest_kernel,
        (partial, low, high, w_far),
        [VMEM] * 4,
        (jax.ShapeDtypeStruct((rows, wide), BF16), jax.ShapeDtypeStruct((1, rows), F32)),
        [],
        1.5,
        mib=14,
    )


def pool_kernel(width, h, square, packed, packed_other, mask, out):
    rows, wide = h.shape
    entries = packed.shape[0] - 16
    scale = jnp.broadcast_to(lax.rsqrt(square[...] / width + EPS), (HEAD, rows)).T
    keep = jnp.broadcast_to(mask[...], (HEAD, rows)).T
    count = jnp.sum(mask[...], axis=1, keepdims=True)
    heads = wide // HEAD
    for head in range(heads):
        cols = slice(head * HEAD, (head + 1) * HEAD)
        held = packed if head < heads // 2 else packed_other
        start = head % (heads // 2) * HEAD
        gain = held[entries : entries + 1, start : start + HEAD].astype(F32)
        block = (h[:, cols].astype(F32) * scale * gain).astype(BF16)
        lat = held[:entries, start : start + HEAD]
        logits = lax.dot_general(lat, block, NT, preferred_element_type=F32)
        top = jnp.max(logits, axis=0, keepdims=True)
        power = jnp.exp2((logits - top) * EXPONENT)
        share = mask[...] / jnp.sum(power, axis=0, keepdims=True)
        power = power * share
        folded = power[:, :HEAD]
        for k in range(1, rows // HEAD):
            folded = folded + power[:, k * HEAD : (k + 1) * HEAD]
        taken = jnp.sum(folded, axis=1, keepdims=True)
        cross = jnp.sum(taken * lat.astype(F32), axis=0, keepdims=True)
        kept = jnp.sum(block.astype(F32) * keep, axis=0, keepdims=True)
        out[:, cols] = (cross + kept) / count


def pool(h, square, packed, packed_other, mask):
    rows, wide = h.shape

    def kernel(*refs):
        pool_kernel(4 * wide, *refs)

    return call(
        kernel,
        (h, square, packed, packed_other, mask),
        [VMEM] * 5,
        jax.ShapeDtypeStruct((1, wide), F32),
        [],
        3.5,
        mib=14,
    )


def turn_kernel(at, queries, out, held, sem):
    count = out.shape[1]
    start = pl.multiple_of(at[0] * count, count)
    copy = pltpu.make_async_copy(queries.at[pl.ds(start, count)], held, sem.at[0])
    copy.start()
    copy.wait()
    out[...] = held[...].T


def turn(at, queries, count):
    part = queries.shape[1]
    return call(
        turn_kernel,
        (at, queries),
        [SMEM, HBM],
        jax.ShapeDtypeStruct((part, count), BF16),
        [pltpu.VMEM((count, part), BF16), pltpu.SemaphoreType.DMA((1,))],
        2.0,
        mib=58,
    )


def score_kernel(every, norms, *refs):
    parts, out = refs[:-1], refs[-1]
    tile = parts[0].shape[1]
    count = tile * len(parts)
    block = every[...]
    values = block.astype(F32)
    square = jnp.sum(values * values, axis=1, keepdims=True)
    out[:, count : count + HEAD] = jnp.broadcast_to(square, (block.shape[0], HEAD))
    out[: norms.shape[0], count + HEAD :] = norms[...]
    out[norms.shape[0] :, count + HEAD :] = jnp.zeros_like(norms)
    for k, held in enumerate(parts):
        out[:, k * tile : (k + 1) * tile] = jnp.dot(
            block, held[...], preferred_element_type=F32
        )


def score(every, norms, parts):
    passages = every.shape[0]
    count = parts[0].shape[1] * len(parts)
    return call(
        score_kernel,
        (every, norms, *parts),
        [VMEM] * (2 + len(parts)),
        jax.ShapeDtypeStruct((passages, count + 2 * HEAD), F32),
        [],
        1.0,
        mib=10,
    )


def merge_kernel(mine, other, out):
    wide = out.shape[1]
    count = wide - 4 * HEAD
    total = mine[...] + other[...]
    rest = total[:, count:]
    high = rest.astype(BF16)
    out[:, :count] = total[:, :count].astype(BF16)
    out[:, count : count + 2 * HEAD] = high
    out[:, count + 2 * HEAD :] = (rest - high.astype(F32)).astype(BF16)


def merge(mine, other):
    passages, wide = mine.shape
    return call(
        merge_kernel,
        (mine, other),
        [VMEM] * 2,
        jax.ShapeDtypeStruct((passages, wide + 2 * HEAD), BF16),
        [],
        0.6,
        mib=6,
    )


def finish_kernel(mine, other, similarity, log_norm):
    count = similarity.shape[1]
    total = mine[...].astype(F32) + other[...].astype(F32)
    rest = total[:, count : count + 2 * HEAD] + total[:, count + 2 * HEAD :]
    scale = lax.rsqrt(rest[:, :1] + 1e-06) / logit_divisor
    norms = [rest[k : k + 1, HEAD:] for k in range(count // HEAD)]
    scores = total[:, :count] * scale * lax.rsqrt(jnp.concatenate(norms, axis=1) + 1e-06)
    similarity[...] = scores
    top = jnp.max(scores, axis=0, keepdims=True)
    log_norm[...] = top + jnp.log(jnp.sum(jnp.exp(scores - top), axis=0, keepdims=True))


def finish(mine, other):
    passages, wide = mine.shape
    count = wide - 4 * HEAD
    return call(
        finish_kernel,
        (mine, other),
        [VMEM] * 2,
        (
            jax.ShapeDtypeStruct((passages, count), F32),
            jax.ShapeDtypeStruct((1, count), F32),
        ),
        [],
        0.8,
        mib=6,
    )


def local(
    hidden_in, norm_gain, w_query, w_key, w_value, w_out, final_gain, latents, token_mask, queries
):
    length, part_width = hidden_in.shape[1:]
    part = part_width // 2
    dp, tensor = lax.axis_index("dp"), lax.axis_index("tensor")
    y, x_hi, z = dp // 8, (dp // 4) % 2, dp % 4
    x_lo, core = tensor // 2, tensor % 2
    at = jnp.stack([y, x_hi, z, x_lo, core]).astype(jnp.int32)

    def halves(side):
        taken = []
        for weights in (w_query, w_key, w_value):
            wide = weights.shape[1] // 2
            taken.append(lax.dynamic_slice_in_dim(weights, side * wide, wide, 1))
        return jnp.concatenate(taken, axis=1)

    half = HEAD // 2
    freqs = 10000.0 ** (-2.0 * jnp.arange(half, dtype=F32) / HEAD)
    angle = jnp.arange(length, dtype=F32)[:, None] * freqs[None, :]
    cosine = jnp.concatenate([jnp.cos(angle), jnp.cos(angle)], axis=1)
    sine = jnp.concatenate([-jnp.sin(angle), jnp.sin(angle)], axis=1)

    hidden = hidden_in[0]
    hidden_other = move(hidden, lambda y, a, z, b, c: (y, a, z, b, a), lambda y, a, z, b, c: c != a)
    whole = jnp.concatenate([hidden, hidden_other], axis=0)
    lat = lax.dynamic_slice_in_dim(latents, x_hi * part, part, 1)
    gain = lax.dynamic_slice_in_dim(final_gain, x_hi * part, part, 0)
    packed = jnp.concatenate([lat, jnp.broadcast_to(gain[None], (16, part))], axis=0)
    packed_other = swap_core(packed)
    q_f = queries.astype(F32)
    norms = jnp.sum(q_f * q_f, -1).reshape(-1, HEAD)

    theirs = halves(1 - x_hi)
    deep, wide = theirs.shape
    row = jnp.pad(token_mask.astype(BF16), ((0, 15), (0, wide - length)))
    theirs = swap_x_hi(jnp.concatenate([theirs, row], axis=0))
    mask_other = theirs[deep : deep + 1, :length].astype(jnp.int32)
    whole = behind(whole, theirs, norms, packed_other)
    x_before = move(whole, along_x(1), holds(0))
    x_after = move(whole, along_x(-1), holds(0))

    shard = jnp.concatenate([halves(x_hi), theirs[:deep]], axis=0)
    line = jnp.concatenate(direct(shard, first_leg), axis=0)
    w_before, w_after = near(line, second_leg)
    line_other = swap_core(line)
    there = line_other[:1, :1]
    x_low, x_high = halves_of(behind(x_before, there), behind(x_after, there))
    x_low = move(x_low, along_x(1), holds(-1))
    x_high = move(x_high, along_x(-1), holds(1))
    low, high = halves_of(w_before, w_after)
    w_low, w_high = far(low, high, second_leg)
    w_before_other = swap_core(w_before)
    w_after_other = swap_core(w_after)

    own, other, residual = normalize(
        at, (whole, x_before, x_after, x_low, x_high), norm_gain[None].astype(F32)
    )
    partial, projected = project_part(
        own, other, (line, w_before, w_after), (line_other, w_before_other, w_after_other)
    )

    mask = jnp.where(x_hi == core, token_mask, mask_other)
    bias = jnp.where(mask[0][:, None] > 0, 0.0, -1e30).astype(F32)
    bias = jnp.broadcast_to(bias, (length, HEAD))
    mask = mask.astype(F32)
    w_pieces = (w_low, w_high, swap_core(w_low), swap_core(w_high))
    cosine = behind(cosine, projected)
    attended, seen = attend(partial, own, other, w_pieces, cosine, sine, bias)
    a_before, a_after = near(attended, along_x)

    block = move(w_out, lambda y, a, z, b, c: (2 * b + c, a, z, y // 2, y % 2))
    out_blocks = direct(behind(block, projected), first_leg)
    out_line = jnp.concatenate([behind(piece, seen) for piece in out_blocks], axis=0)
    out_pieces = direct(out_line, second_leg)
    out_others = tuple(swap_core(piece) for piece in out_pieces)

    a_low, a_high = halves_of(behind(a_before, a_after), behind(a_after, a_before))
    a_low, a_high = far(a_low, a_high, along_x)
    partial, w_out_far = output_part(
        at,
        (attended, a_before, a_after),
        out_pieces,
        out_others,
        residual,
    )
    h, square = output_rest(partial, w_out_far, a_low, a_high)
    parts = 4
    turned = [
        turn(behind(jnp.full((1,), k, jnp.int32), square), queries, queries.shape[0] // parts)
        for k in range(parts)
    ]
    square = square + swap_x_lo(square)
    square = square + swap_x_next(square)
    pooled = pool(h, square, packed, packed_other, mask)

    def in_order(first, values, other, axis):
        low, high = jnp.where(first, values, other), jnp.where(first, other, values)
        return jnp.concatenate([low, high], axis=axis)

    emb = pooled.astype(BF16)
    emb = in_order(core == 0, emb[:, :part], swap_core(emb[:, part:]), 0)
    emb = in_order(x_hi == 0, emb, swap_x_hi(emb), 1)
    emb = emb[None, :, None]
    emb = in_order(z % 2 == 0, emb, move(emb, lambda y, a, z, b, c: (y, a, z ^ 1, b, c)), 2)
    emb = in_order(z < 2, emb, move(emb, lambda y, a, z, b, c: (y, a, 3 - z, b, c)), 2)
    emb = in_order(y % 2 == 0, emb, move(emb, lambda y, a, z, b, c: (y ^ 1, a, z, b, c)), 0)
    emb = in_order(y < 2, emb, move(emb, lambda y, a, z, b, c: (3 - y, a, z, b, c)), 0)
    products = score(emb.reshape(32, part_width), norms, turned)
    products = merge(products, swap_core(products))
    similarity, log_norm = finish(products, swap_x_lo(products))
    return (similarity.T, log_norm[0])


def solution(mesh):
    placed = (
        P("dp", None, "tensor"),
        P(),
        P("dp", "tensor"),
        P("dp", "tensor"),
        P("dp", "tensor"),
        P("tensor", "dp"),
        P("tensor"),
        P(None, "tensor"),
        P("dp", None),
        P("dp", "tensor"),
    )
    return jax.shard_map(
        local, mesh=mesh, in_specs=placed, out_specs=(P("dp", None), P("dp")), check_vma=False
    )
```

```python
import jax
import jax.numpy as jnp
from jax import lax
from jax.experimental import pallas as pl
from jax.experimental.pallas import tpu as pltpu
from jax.sharding import PartitionSpec as P

HEAD = 128
EPS = 1e-05
logit_divisor = 0.02
BOTH = ("dp", "tensor")
COORDS = [
    (y, a, z, b, c)
    for y in range(4)
    for a in range(2)
    for z in range(4)
    for b in range(2)
    for c in range(2)
]


def index_of(y, a, z, b, c):
    return (((y * 2 + a) * 4 + z) * 2 + b) * 2 + c


def move(values, where, when=lambda *at: True):
    pairs = [(index_of(*at), index_of(*where(*at))) for at in COORDS if when(*at)]
    return lax.ppermute(values, BOTH, pairs)


def swap_core(values):
    return move(values, lambda y, a, z, b, c: (y, a, z, b, 1 - c))


def swap_x_hi(values):
    return move(values, lambda y, a, z, b, c: (y, 1 - a, z, b, c))


def swap_x_lo(values):
    return move(values, lambda y, a, z, b, c: (y, a, z, 1 - b, c))


def swap_x_next(values):
    return move(values, lambda y, a, z, b, c: (y, 1 - a, z, 1 - b, c))


def along_x(step):
    def where(y, a, z, b, c):
        x = (2 * a + b + step) % 4
        return (y, x // 2, z, x % 2, c)

    return where


def first_leg(step):
    def where(y, a, z, b, c):
        if c == 0:
            return ((y + step) % 4, a, z, b, c)
        return (y, a, (z + step) % 4, b, c)

    return where


def second_leg(step):
    def where(y, a, z, b, c):
        if c == 0:
            return (y, a, (z + step) % 4, b, c)
        return ((y + step) % 4, a, z, b, c)

    return where


def near(values, leg):
    return move(values, leg(1)), move(values, leg(-1))


def halves_of(before, after):
    half = before.shape[0] // 2
    return before[:half], after[half:]


def far(low, high, leg):
    return move(low, leg(1)), move(high, leg(-1))


def direct(values, leg):
    return values, move(values, leg(1)), move(values, leg(-1)), move(values, leg(2))


def holds(step):
    def when(y, a, z, b, c):
        return (2 * a + b + step) % 4 // 2 == c

    return when


def behind(values, *others):
    return lax.optimization_barrier((values,) + others)[0]


AT_Y, AT_X_HI, AT_Z, AT_X_LO, AT_CORE = range(5)
VMEM = pl.BlockSpec(memory_space=pltpu.VMEM)
SMEM = pl.BlockSpec(memory_space=pltpu.SMEM)
HBM = pl.BlockSpec(memory_space=pltpu.HBM)
F32, BF16 = jnp.float32, jnp.bfloat16
OFFSETS = (0, 3, 1, 2)
NT = (((1,), (1,)), ((), ()))
RATE = 1.15e9
EXPONENT = HEAD ** (-0.5) * 1.4426950408889634


def call(kernel, args, specs, out, scratch, micros, mib=48):
    return pl.pallas_call(
        kernel,
        out_shape=out,
        in_specs=specs,
        out_specs=jax.tree.map(lambda _: VMEM, out),
        scratch_shapes=scratch,
        compiler_params=pltpu.CompilerParams(vmem_limit_bytes=mib * 1024 * 1024),
        cost_estimate=pl.CostEstimate(
            flops=int(micros * RATE), bytes_accessed=1024, transcendentals=0
        ),
    )(*args)


def leg_positions(at, core, first, second):
    y = jnp.where(core == 0, at[AT_Y] + first, at[AT_Y] + second) % 4
    z = jnp.where(core == 0, at[AT_Z] + second, at[AT_Z] + first) % 4
    return y, z


def norm_kernel(at, *refs):
    whole, before, after, low, high, gain, own, other, residual, done, tokens, sems = refs
    rows, part = low.shape
    done[...] = jnp.zeros_like(done)
    a, b, core = at[AT_X_HI], at[AT_X_LO], at[AT_CORE]
    here = a == core
    near = jnp.logical_or(
        jnp.logical_and(here, b == 0), jnp.logical_and(jnp.logical_not(here), b == 1)
    )

    def send(src, block, sem):
        column = pl.multiple_of(block * part, part)
        return pltpu.make_async_copy(src, tokens.at[:, pl.ds(column, part)], sems.at[sem])

    first, second = 2 * b + core, 2 * b + 1 - core
    third, fourth = 2 * (1 - b) + core, 2 * (1 - b) + 1 - core

    @pl.when(here)
    def _():
        send(whole.at[pl.ds(0, rows)], first, 0).start()
        send(whole.at[pl.ds(rows, rows)], second, 1).start()

    @pl.when(jnp.logical_not(here))
    def _():
        send(low, first, 0).start()
        send(high, second, 1).start()

    @pl.when(near)
    def _():
        send(after.at[pl.ds(0, rows)], third, 2).start()
        send(after.at[pl.ds(rows, rows)], fourth, 3).start()

    @pl.when(jnp.logical_not(near))
    def _():
        send(before.at[pl.ds(0, rows)], third, 2).start()
        send(before.at[pl.ds(rows, rows)], fourth, 3).start()

    for sem in range(4):
        send(low, 0, sem).wait()

    own_columns = part // 2
    for k, held in enumerate((first, second)):
        lane = pl.multiple_of(held * part + a * own_columns, own_columns)
        residual[:, k * own_columns : (k + 1) * own_columns] = tokens[:, pl.ds(lane, own_columns)]

    width = tokens.shape[1]
    tile = 64
    lanes = []
    for two, later in enumerate(OFFSETS):
        for one, sooner in enumerate(OFFSETS):
            y, z = leg_positions(at, core, sooner, later)
            for entry in range(2):
                lane = pl.multiple_of((y * 8 + (a + entry) % 2 * 4 + z) * HEAD, HEAD)
                mine = ((two * 4 + one) * 2 + entry) * HEAD
                turned = ((one * 4 + two) * 2 + entry) * HEAD
                lanes.append((pl.ds(lane, HEAD), mine, turned))

    @pl.loop(0, rows // tile)
    def _(step):
        at_rows = pl.ds(pl.multiple_of(step * tile, tile), tile)
        squares = jnp.zeros((tile, HEAD), F32)
        for lane in range(0, width, HEAD):
            values = tokens[at_rows, lane : lane + HEAD].astype(F32)
            squares = squares + values * values
        mean = jnp.sum(squares, axis=-1, keepdims=True) / width
        scale = jnp.broadcast_to(lax.rsqrt(mean + EPS), (tile, HEAD))
        for lane, mine, turned in lanes:
            values = tokens[at_rows, lane].astype(F32) * scale * gain[:, lane]
            values = values.astype(BF16)
            own[at_rows, mine : mine + HEAD] = values
            other[at_rows, turned : turned + HEAD] = values


def normalize(at, hidden, gain):
    rows, part = hidden[3].shape
    width = gain.shape[1]
    return call(
        norm_kernel,
        (at, *hidden, gain),
        [SMEM] + [HBM] * 5 + [VMEM],
        (
            jax.ShapeDtypeStruct((rows, width), BF16),
            jax.ShapeDtypeStruct((rows, width), BF16),
            jax.ShapeDtypeStruct((rows, part), BF16),
            jax.ShapeDtypeStruct((8, HEAD), F32),
        ),
        [pltpu.VMEM((rows, width), BF16), pltpu.SemaphoreType.DMA((4,))],
        30.0,
        mib=16,
    )


def project_kernel(own, other, *refs):
    lines, total = refs[:6], refs[6]
    deep, wide = lines[0].shape
    for k, normed in enumerate((own, other)):
        total[:, k * wide : (k + 1) * wide] = sum(
            jnp.dot(
                normed[:, j * deep : (j + 1) * deep],
                lines[3 * k + j][...],
                preferred_element_type=F32,
            )
            for j in range(3)
        )


def project_part(own, other, lines, others):
    rows = own.shape[0]
    wide = lines[0].shape[1]
    return call(
        project_kernel,
        (own, other, *lines, *others),
        [VMEM] * 8,
        jax.ShapeDtypeStruct((rows, 2 * wide), F32),
        [],
        7.0,
        mib=20,
    )


def attention_kernel(partial, own, other, *refs):
    pieces, (cosine, sine, bias, out, done, total, qkv) = refs[:4], refs[4:]
    done[...] = jnp.zeros_like(done)
    rows = partial.shape[0]
    half = pieces[0].shape[0]
    wide = partial.shape[1] // 2
    heads = wide // HEAD - 2
    for k, normed in enumerate((own, other)):
        base = k * wide
        start = normed.shape[1] - 2 * half
        total[...] = (
            partial[:, base : base + wide]
            + jnp.dot(
                normed[:, start : start + half], pieces[2 * k][...], preferred_element_type=F32
            )
            + jnp.dot(
                normed[:, start + half :], pieces[2 * k + 1][...], preferred_element_type=F32
            )
        )
        for head in range(heads + 1):
            cols = slice(head * HEAD, (head + 1) * HEAD)
            block = total[:, cols]
            turned = block * cosine[...] + pltpu.roll(block, HEAD // 2, 1) * sine[...]
            qkv[:, cols] = turned.astype(BF16)
        keys = qkv[:, heads * HEAD : (heads + 1) * HEAD]
        values_t = total[:, (heads + 1) * HEAD :].T.astype(BF16)
        for head in range(heads):
            query = qkv[:, head * HEAD : (head + 1) * HEAD]
            logits = lax.dot_general(keys, query, NT, preferred_element_type=F32)
            logits = logits + jnp.concatenate([bias[...]] * (rows // HEAD), axis=1)
            top = jnp.max(logits, axis=0, keepdims=True)
            power = jnp.exp2((logits - top) * EXPONENT)
            share = 1.0 / jnp.sum(power, axis=0, keepdims=True)
            mixed = jnp.dot(values_t, power.astype(BF16), preferred_element_type=F32)
            start = (k * heads + head) * HEAD
            out[:, start : start + HEAD] = (mixed * share).T.astype(BF16)


def attend(partial, own, other, pieces, cosine, sine, bias):
    rows, wide = partial.shape
    heads = wide // HEAD - 4
    return call(
        attention_kernel,
        (partial, own, other, *pieces, cosine, sine, bias),
        [VMEM] * 10,
        (jax.ShapeDtypeStruct((rows, heads * HEAD), BF16), jax.ShapeDtypeStruct((8, HEAD), F32)),
        [pltpu.VMEM((rows, wide // 2), F32), pltpu.VMEM((rows, wide // 2), BF16)],
        8.0,
        mib=20,
    )


def output_kernel(at, *refs):
    attended, blocks, others = refs[:3], refs[3:7], refs[7:11]
    residual, partial, w_far, weights, sems = refs[11:]
    rows, wide = attended[0].shape
    part = wide // 2
    count = weights.shape[0] // 4
    a, b, core = at[AT_X_HI], at[AT_X_LO], at[AT_CORE]
    copies = []
    for two, second in enumerate(OFFSETS):
        for one, first in enumerate(OFFSETS):
            for k, (held, leg_core) in enumerate(((blocks, core), (others, 1 - core))):
                y, z = leg_positions(at, leg_core, first, second)
                column = pl.multiple_of(k * part + z * HEAD, HEAD)
                copies.append(
                    pltpu.make_async_copy(
                        held[two].at[pl.ds(one * count, count)],
                        weights.at[
                            pl.ds(pl.multiple_of(y * count, count), count), pl.ds(column, HEAD)
                        ],
                        sems.at[len(copies)],
                    )
                )
    for copy in copies:
        copy.start()
    for copy in copies:
        copy.wait()

    def held_rows(offset, k):
        chip = (2 * a + b + offset) % 4
        there = core if k == 0 else 1 - core
        row = ((chip % 2 * 2 + there) * 2 + chip // 2) * part
        return weights[pl.ds(pl.multiple_of(row, part), part), :]

    for k in range(2):
        w_far[k * part : (k + 1) * part, :] = held_rows(2, k)
    partial[...] = residual[...].astype(F32)
    for piece, offset in zip(attended, OFFSETS[:3], strict=True):
        for k in range(2):
            partial[...] += jnp.dot(
                piece[:, k * part : (k + 1) * part],
                held_rows(offset, k),
                preferred_element_type=F32,
            )


def output_part(at, attended, blocks, others, residual):
    rows, wide = attended[0].shape
    width = blocks[0].shape[0]
    return call(
        output_kernel,
        (at, *attended, *blocks, *others, residual),
        [SMEM] + [VMEM] * 3 + [HBM] * 8 + [VMEM],
        (jax.ShapeDtypeStruct((rows, wide), F32), jax.ShapeDtypeStruct((wide, wide), BF16)),
        [
            pltpu.VMEM((width, wide), BF16),
            pltpu.SemaphoreType.DMA((32,)),
        ],
        9.5,
        mib=28,
    )


def output_rest_kernel(partial, low, high, w_far, h, square):
    half, wide = low.shape
    for k, piece in enumerate((low, high)):
        at_rows = slice(k * half, (k + 1) * half)
        product = jnp.dot(piece[...], w_far[...], preferred_element_type=F32)
        block = (partial[at_rows, :] + product).astype(BF16)
        h[at_rows, :] = block
        block = block.astype(F32)
        block = block * block
        folded = block[:, :HEAD]
        for lane in range(HEAD, wide, HEAD):
            folded = folded + block[:, lane : lane + HEAD]
        square[:, at_rows] = jnp.sum(folded.T, axis=0, keepdims=True)


def output_rest(partial, w_far, low, high):
    rows, wide = partial.shape
    return call(
        output_rest_kernel,
        (partial, low, high, w_far),
        [VMEM] * 4,
        (jax.ShapeDtypeStruct((rows, wide), BF16), jax.ShapeDtypeStruct((1, rows), F32)),
        [],
        1.5,
        mib=14,
    )


def pool_kernel(width, h, square, packed, packed_other, mask, out):
    rows, wide = h.shape
    entries = packed.shape[0] - 16
    scale = jnp.broadcast_to(lax.rsqrt(square[...] / width + EPS), (HEAD, rows)).T
    keep = jnp.broadcast_to(mask[...], (HEAD, rows)).T
    count = jnp.sum(mask[...], axis=1, keepdims=True)
    heads = wide // HEAD
    for head in range(heads):
        cols = slice(head * HEAD, (head + 1) * HEAD)
        held = packed if head < heads // 2 else packed_other
        start = head % (heads // 2) * HEAD
        gain = held[entries : entries + 1, start : start + HEAD].astype(F32)
        block = (h[:, cols].astype(F32) * scale * gain).astype(BF16)
        lat = held[:entries, start : start + HEAD]
        logits = lax.dot_general(lat, block, NT, preferred_element_type=F32)
        top = jnp.max(logits, axis=0, keepdims=True)
        power = jnp.exp2((logits - top) * EXPONENT)
        share = mask[...] / jnp.sum(power, axis=0, keepdims=True)
        power = power * share
        folded = power[:, :HEAD]
        for k in range(1, rows // HEAD):
            folded = folded + power[:, k * HEAD : (k + 1) * HEAD]
        taken = jnp.sum(folded, axis=1, keepdims=True)
        cross = jnp.sum(taken * lat.astype(F32), axis=0, keepdims=True)
        kept = jnp.sum(block.astype(F32) * keep, axis=0, keepdims=True)
        out[:, cols] = (cross + kept) / count


def pool(h, square, packed, packed_other, mask):
    rows, wide = h.shape

    def kernel(*refs):
        pool_kernel(4 * wide, *refs)

    return call(
        kernel,
        (h, square, packed, packed_other, mask),
        [VMEM] * 5,
        jax.ShapeDtypeStruct((1, wide), F32),
        [],
        3.5,
        mib=14,
    )


def turn_kernel(at, queries, out, held, sem):
    count = out.shape[1]
    start = pl.multiple_of(at[0] * count, count)
    copy = pltpu.make_async_copy(queries.at[pl.ds(start, count)], held, sem.at[0])
    copy.start()
    copy.wait()
    out[...] = held[...].T


def turn(at, queries, count):
    part = queries.shape[1]
    return call(
        turn_kernel,
        (at, queries),
        [SMEM, HBM],
        jax.ShapeDtypeStruct((part, count), BF16),
        [pltpu.VMEM((count, part), BF16), pltpu.SemaphoreType.DMA((1,))],
        2.0,
        mib=58,
    )


def score_kernel(every, norms, *refs):
    parts, out = refs[:-1], refs[-1]
    tile = parts[0].shape[1]
    count = tile * len(parts)
    block = every[...]
    values = block.astype(F32)
    square = jnp.sum(values * values, axis=1, keepdims=True)
    out[:, count : count + HEAD] = jnp.broadcast_to(square, (block.shape[0], HEAD))
    out[: norms.shape[0], count + HEAD :] = norms[...]
    out[norms.shape[0] :, count + HEAD :] = jnp.zeros_like(norms)
    for k, held in enumerate(parts):
        out[:, k * tile : (k + 1) * tile] = jnp.dot(
            block, held[...], preferred_element_type=F32
        )


def score(every, norms, parts):
    passages = every.shape[0]
    count = parts[0].shape[1] * len(parts)
    return call(
        score_kernel,
        (every, norms, *parts),
        [VMEM] * (2 + len(parts)),
        jax.ShapeDtypeStruct((passages, count + 2 * HEAD), F32),
        [],
        1.0,
        mib=10,
    )


def merge_kernel(mine, other, out):
    wide = out.shape[1]
    count = wide - 4 * HEAD
    total = mine[...] + other[...]
    rest = total[:, count:]
    high = rest.astype(BF16)
    out[:, :count] = total[:, :count].astype(BF16)
    out[:, count : count + 2 * HEAD] = high
    out[:, count + 2 * HEAD :] = (rest - high.astype(F32)).astype(BF16)


def merge(mine, other):
    passages, wide = mine.shape
    return call(
        merge_kernel,
        (mine, other),
        [VMEM] * 2,
        jax.ShapeDtypeStruct((passages, wide + 2 * HEAD), BF16),
        [],
        0.6,
        mib=6,
    )


def finish_kernel(mine, other, similarity, log_norm):
    count = similarity.shape[1]
    total = mine[...].astype(F32) + other[...].astype(F32)
    rest = total[:, count : count + 2 * HEAD] + total[:, count + 2 * HEAD :]
    scale = lax.rsqrt(rest[:, :1] + 1e-06) / logit_divisor
    norms = [rest[k : k + 1, HEAD:] for k in range(count // HEAD)]
    scores = total[:, :count] * scale * lax.rsqrt(jnp.concatenate(norms, axis=1) + 1e-06)
    similarity[...] = scores
    top = jnp.max(scores, axis=0, keepdims=True)
    log_norm[...] = top + jnp.log(jnp.sum(jnp.exp(scores - top), axis=0, keepdims=True))


def finish(mine, other):
    passages, wide = mine.shape
    count = wide - 4 * HEAD
    return call(
        finish_kernel,
        (mine, other),
        [VMEM] * 2,
        (
            jax.ShapeDtypeStruct((passages, count), F32),
            jax.ShapeDtypeStruct((1, count), F32),
        ),
        [],
        0.8,
        mib=6,
    )


def local(
    hidden_in, norm_gain, w_query, w_key, w_value, w_out, final_gain, latents, token_mask, queries
):
    length, part_width = hidden_in.shape[1:]
    part = part_width // 2
    dp, tensor = lax.axis_index("dp"), lax.axis_index("tensor")
    y, x_hi, z = dp // 8, (dp // 4) % 2, dp % 4
    x_lo, core = tensor // 2, tensor % 2
    at = jnp.stack([y, x_hi, z, x_lo, core]).astype(jnp.int32)

    def halves(side):
        taken = []
        for weights in (w_query, w_key, w_value):
            wide = weights.shape[1] // 2
            taken.append(lax.dynamic_slice_in_dim(weights, side * wide, wide, 1))
        return jnp.concatenate(taken, axis=1)

    half = HEAD // 2
    freqs = 10000.0 ** (-2.0 * jnp.arange(half, dtype=F32) / HEAD)
    angle = jnp.arange(length, dtype=F32)[:, None] * freqs[None, :]
    cosine = jnp.concatenate([jnp.cos(angle), jnp.cos(angle)], axis=1)
    sine = jnp.concatenate([-jnp.sin(angle), jnp.sin(angle)], axis=1)

    hidden = hidden_in[0]
    hidden_other = move(hidden, lambda y, a, z, b, c: (y, a, z, b, a), lambda y, a, z, b, c: c != a)
    whole = jnp.concatenate([hidden, hidden_other], axis=0)
    lat = lax.dynamic_slice_in_dim(latents, x_hi * part, part, 1)
    gain = lax.dynamic_slice_in_dim(final_gain, x_hi * part, part, 0)
    packed = jnp.concatenate([lat, jnp.broadcast_to(gain[None], (16, part))], axis=0)
    packed_other = swap_core(packed)
    q_f = queries.astype(F32)
    norms = jnp.sum(q_f * q_f, -1).reshape(-1, HEAD)

    theirs = halves(1 - x_hi)
    deep, wide = theirs.shape
    row = jnp.pad(token_mask.astype(BF16), ((0, 15), (0, wide - length)))
    theirs = swap_x_hi(jnp.concatenate([theirs, row], axis=0))
    mask_other = theirs[deep : deep + 1, :length].astype(jnp.int32)
    whole = behind(whole, theirs, norms, packed_other)
    x_before = move(whole, along_x(1), holds(0))
    x_after = move(whole, along_x(-1), holds(0))

    shard = jnp.concatenate([halves(x_hi), theirs[:deep]], axis=0)
    shard = behind(shard, norms, packed_other)
    line = jnp.concatenate(direct(shard, first_leg), axis=0)
    w_before, w_after = near(line, second_leg)
    line_other = swap_core(line)
    there = line_other[:1, :1]
    x_low, x_high = halves_of(behind(x_before, there), behind(x_after, there))
    x_low = move(x_low, along_x(1), holds(-1))
    x_high = move(x_high, along_x(-1), holds(1))
    low, high = halves_of(w_before, w_after)
    w_low, w_high = far(low, high, second_leg)
    w_before_other = swap_core(w_before)
    w_after_other = swap_core(w_after)

    own, other, residual, scaled = normalize(
        at, (whole, x_before, x_after, x_low, x_high), norm_gain[None].astype(F32)
    )
    partial = project_part(
        own, other, (line, w_before, w_after), (line_other, w_before_other, w_after_other)
    )

    mask = jnp.where(x_hi == core, token_mask, mask_other)
    bias = jnp.where(mask[0][:, None] > 0, 0.0, -1e30).astype(F32)
    bias = jnp.broadcast_to(bias, (length, HEAD))
    mask = mask.astype(F32)
    w_pieces = (w_low, w_high, swap_core(w_low), swap_core(w_high))
    projected = partial[:1, :1]
    cosine = behind(cosine, projected, scaled)
    attended, seen = attend(partial, own, other, w_pieces, cosine, sine, bias)
    a_before, a_after = near(attended, along_x)

    block = move(behind(w_out, scaled), lambda y, a, z, b, c: (2 * b + c, a, z, y // 2, y % 2))
    out_blocks = direct(behind(block, projected), first_leg)
    out_line = jnp.concatenate([behind(piece, seen) for piece in out_blocks], axis=0)
    out_pieces = direct(out_line, second_leg)
    out_others = tuple(swap_core(piece) for piece in out_pieces)

    a_low, a_high = halves_of(a_before, a_after)
    a_low, a_high = far(a_low, a_high, along_x)
    partial, w_out_far = output_part(
        at,
        (attended, a_before, a_after),
        out_pieces,
        out_others,
        residual,
    )
    h, square = output_rest(partial, w_out_far, a_low, a_high)
    parts = 4
    turned = [
        turn(behind(jnp.full((1,), k, jnp.int32), square), queries, queries.shape[0] // parts)
        for k in range(parts)
    ]
    square = square + swap_x_lo(square)
    square = square + swap_x_next(square)
    pooled = pool(h, square, packed, packed_other, mask)

    def in_order(first, values, other, axis):
        low, high = jnp.where(first, values, other), jnp.where(first, other, values)
        return jnp.concatenate([low, high], axis=axis)

    emb = pooled.astype(BF16)
    emb = in_order(core == 0, emb[:, :part], swap_core(emb[:, part:]), 0)
    emb = in_order(x_hi == 0, emb, swap_x_hi(emb), 1)
    emb = emb[None, :, None]
    emb = in_order(z % 2 == 0, emb, move(emb, lambda y, a, z, b, c: (y, a, z ^ 1, b, c)), 2)
    emb = in_order(z < 2, emb, move(emb, lambda y, a, z, b, c: (y, a, 3 - z, b, c)), 2)
    emb = in_order(y % 2 == 0, emb, move(emb, lambda y, a, z, b, c: (y ^ 1, a, z, b, c)), 0)
    emb = in_order(y < 2, emb, move(emb, lambda y, a, z, b, c: (3 - y, a, z, b, c)), 0)
    products = score(emb.reshape(32, part_width), norms, turned)
    products = merge(products, swap_core(products))
    similarity, log_norm = finish(products, swap_x_lo(products))
    return (similarity.T, log_norm[0])


def solution(mesh):
    placed = (
        P("dp", None, "tensor"),
        P(),
        P("dp", "tensor"),
        P("dp", "tensor"),
        P("dp", "tensor"),
        P("tensor", "dp"),
        P("tensor"),
        P(None, "tensor"),
        P("dp", None),
        P("dp", "tensor"),
    )
    return jax.shard_map(
        local, mesh=mesh, in_specs=placed, out_specs=(P("dp", None), P("dp")), check_vma=False
    )
```

```python
import jax
import jax.numpy as jnp
from jax import lax
from jax.experimental import pallas as pl
from jax.experimental.pallas import tpu as pltpu
from jax.sharding import PartitionSpec as P

HEAD = 128
EPS = 1e-05
logit_divisor = 0.02
BOTH = ("dp", "tensor")
COORDS = [
    (y, a, z, b, c)
    for y in range(4)
    for a in range(2)
    for z in range(4)
    for b in range(2)
    for c in range(2)
]


def index_of(y, a, z, b, c):
    return (((y * 2 + a) * 4 + z) * 2 + b) * 2 + c


def move(values, where, when=lambda *at: True):
    pairs = [(index_of(*at), index_of(*where(*at))) for at in COORDS if when(*at)]
    return lax.ppermute(values, BOTH, pairs)


def swap_core(values):
    return move(values, lambda y, a, z, b, c: (y, a, z, b, 1 - c))


def swap_x_hi(values):
    return move(values, lambda y, a, z, b, c: (y, 1 - a, z, b, c))


def swap_x_lo(values):
    return move(values, lambda y, a, z, b, c: (y, a, z, 1 - b, c))


def swap_x_next(values):
    return move(values, lambda y, a, z, b, c: (y, 1 - a, z, 1 - b, c))


def along_x(step):
    def where(y, a, z, b, c):
        x = (2 * a + b + step) % 4
        return (y, x // 2, z, x % 2, c)

    return where


def first_leg(step):
    def where(y, a, z, b, c):
        if c == 0:
            return ((y + step) % 4, a, z, b, c)
        return (y, a, (z + step) % 4, b, c)

    return where


def second_leg(step):
    def where(y, a, z, b, c):
        if c == 0:
            return (y, a, (z + step) % 4, b, c)
        return ((y + step) % 4, a, z, b, c)

    return where


def near(values, leg):
    return move(values, leg(1)), move(values, leg(-1))


def halves_of(before, after):
    half = before.shape[0] // 2
    return before[:half], after[half:]


def far(low, high, leg):
    return move(low, leg(1)), move(high, leg(-1))


def direct(values, leg):
    return values, move(values, leg(1)), move(values, leg(-1)), move(values, leg(2))


def holds(step):
    def when(y, a, z, b, c):
        return (2 * a + b + step) % 4 // 2 == c

    return when


def behind(values, *others):
    return lax.optimization_barrier((values,) + others)[0]


AT_Y, AT_X_HI, AT_Z, AT_X_LO, AT_CORE = range(5)
VMEM = pl.BlockSpec(memory_space=pltpu.VMEM)
SMEM = pl.BlockSpec(memory_space=pltpu.SMEM)
HBM = pl.BlockSpec(memory_space=pltpu.HBM)
F32, BF16 = jnp.float32, jnp.bfloat16
OFFSETS = (0, 3, 1, 2)
NT = (((1,), (1,)), ((), ()))
RATE = 1.15e9
EXPONENT = HEAD ** (-0.5) * 1.4426950408889634


def call(kernel, args, specs, out, scratch, micros, mib=48):
    return pl.pallas_call(
        kernel,
        out_shape=out,
        in_specs=specs,
        out_specs=jax.tree.map(lambda _: VMEM, out),
        scratch_shapes=scratch,
        compiler_params=pltpu.CompilerParams(vmem_limit_bytes=mib * 1024 * 1024),
        cost_estimate=pl.CostEstimate(
            flops=int(micros * RATE), bytes_accessed=1024, transcendentals=0
        ),
    )(*args)


def leg_positions(at, core, first, second):
    y = jnp.where(core == 0, at[AT_Y] + first, at[AT_Y] + second) % 4
    z = jnp.where(core == 0, at[AT_Z] + second, at[AT_Z] + first) % 4
    return y, z


def norm_kernel(at, *refs):
    whole, before, after, low, high, gain, own, other, residual, done, tokens, sems = refs
    rows, part = low.shape
    done[...] = jnp.zeros_like(done)
    a, b, core = at[AT_X_HI], at[AT_X_LO], at[AT_CORE]
    here = a == core
    near = jnp.logical_or(
        jnp.logical_and(here, b == 0), jnp.logical_and(jnp.logical_not(here), b == 1)
    )

    def send(src, block, sem):
        column = pl.multiple_of(block * part, part)
        return pltpu.make_async_copy(src, tokens.at[:, pl.ds(column, part)], sems.at[sem])

    first, second = 2 * b + core, 2 * b + 1 - core
    third, fourth = 2 * (1 - b) + core, 2 * (1 - b) + 1 - core

    @pl.when(here)
    def _():
        send(whole.at[pl.ds(0, rows)], first, 0).start()
        send(whole.at[pl.ds(rows, rows)], second, 1).start()

    @pl.when(jnp.logical_not(here))
    def _():
        send(low, first, 0).start()
        send(high, second, 1).start()

    @pl.when(near)
    def _():
        send(after.at[pl.ds(0, rows)], third, 2).start()
        send(after.at[pl.ds(rows, rows)], fourth, 3).start()

    @pl.when(jnp.logical_not(near))
    def _():
        send(before.at[pl.ds(0, rows)], third, 2).start()
        send(before.at[pl.ds(rows, rows)], fourth, 3).start()

    for sem in range(4):
        send(low, 0, sem).wait()

    own_columns = part // 2
    for k, held in enumerate((first, second)):
        lane = pl.multiple_of(held * part + a * own_columns, own_columns)
        residual[:, k * own_columns : (k + 1) * own_columns] = tokens[:, pl.ds(lane, own_columns)]

    width = tokens.shape[1]
    tile = 128
    lanes = []
    for two, later in enumerate(OFFSETS):
        for one, sooner in enumerate(OFFSETS):
            y, z = leg_positions(at, core, sooner, later)
            for entry in range(2):
                lane = pl.multiple_of((y * 8 + (a + entry) % 2 * 4 + z) * HEAD, HEAD)
                mine = ((two * 4 + one) * 2 + entry) * HEAD
                turned = ((one * 4 + two) * 2 + entry) * HEAD
                lanes.append((pl.ds(lane, HEAD), mine, turned))

    @pl.loop(0, rows // tile)
    def _(step):
        at_rows = pl.ds(pl.multiple_of(step * tile, tile), tile)
        squares = jnp.zeros((tile, HEAD), F32)
        for lane in range(0, width, HEAD):
            values = tokens[at_rows, lane : lane + HEAD].astype(F32)
            squares = squares + values * values
        mean = jnp.sum(squares, axis=-1, keepdims=True) / width
        scale = jnp.broadcast_to(lax.rsqrt(mean + EPS), (tile, HEAD))
        for lane, mine, turned in lanes:
            values = tokens[at_rows, lane].astype(F32) * scale * gain[:, lane]
            values = values.astype(BF16)
            own[at_rows, mine : mine + HEAD] = values
            other[at_rows, turned : turned + HEAD] = values


def normalize(at, hidden, gain):
    rows, part = hidden[3].shape
    width = gain.shape[1]
    return call(
        norm_kernel,
        (at, *hidden, gain),
        [SMEM] + [HBM] * 5 + [VMEM],
        (
            jax.ShapeDtypeStruct((rows, width), BF16),
            jax.ShapeDtypeStruct((rows, width), BF16),
            jax.ShapeDtypeStruct((rows, part), BF16),
            jax.ShapeDtypeStruct((8, HEAD), F32),
        ),
        [pltpu.VMEM((rows, width), BF16), pltpu.SemaphoreType.DMA((4,))],
        30.0,
        mib=16,
    )


def project_kernel(own, other, *refs):
    lines, total = refs[:6], refs[6]
    deep, wide = lines[0].shape
    for k, normed in enumerate((own, other)):
        total[:, k * wide : (k + 1) * wide] = sum(
            jnp.dot(
                normed[:, j * deep : (j + 1) * deep],
                lines[3 * k + j][...],
                preferred_element_type=F32,
            )
            for j in range(3)
        )


def project_part(own, other, lines, others):
    rows = own.shape[0]
    wide = lines[0].shape[1]
    return call(
        project_kernel,
        (own, other, *lines, *others),
        [VMEM] * 8,
        jax.ShapeDtypeStruct((rows, 2 * wide), F32),
        [],
        7.0,
        mib=20,
    )


def attention_kernel(partial, own, other, *refs):
    pieces, (cosine, sine, bias, out, done, total, qkv) = refs[:4], refs[4:]
    done[...] = jnp.zeros_like(done)
    rows = partial.shape[0]
    half = pieces[0].shape[0]
    wide = partial.shape[1] // 2
    heads = wide // HEAD - 2
    for k, normed in enumerate((own, other)):
        base = k * wide
        start = normed.shape[1] - 2 * half
        total[...] = (
            partial[:, base : base + wide]
            + jnp.dot(
                normed[:, start : start + half], pieces[2 * k][...], preferred_element_type=F32
            )
            + jnp.dot(
                normed[:, start + half :], pieces[2 * k + 1][...], preferred_element_type=F32
            )
        )
        for head in range(heads + 1):
            cols = slice(head * HEAD, (head + 1) * HEAD)
            block = total[:, cols]
            turned = block * cosine[...] + pltpu.roll(block, HEAD // 2, 1) * sine[...]
            qkv[:, cols] = turned.astype(BF16)
        keys = qkv[:, heads * HEAD : (heads + 1) * HEAD]
        values_t = total[:, (heads + 1) * HEAD :].T.astype(BF16)
        for head in range(heads):
            query = qkv[:, head * HEAD : (head + 1) * HEAD]
            logits = lax.dot_general(keys, query, NT, preferred_element_type=F32)
            logits = logits + jnp.concatenate([bias[...]] * (rows // HEAD), axis=1)
            top = jnp.max(logits, axis=0, keepdims=True)
            power = jnp.exp2((logits - top) * EXPONENT)
            share = 1.0 / jnp.sum(power, axis=0, keepdims=True)
            mixed = jnp.dot(values_t, power.astype(BF16), preferred_element_type=F32)
            start = (k * heads + head) * HEAD
            out[:, start : start + HEAD] = (mixed * share).T.astype(BF16)


def attend(partial, own, other, pieces, cosine, sine, bias):
    rows, wide = partial.shape
    heads = wide // HEAD - 4
    return call(
        attention_kernel,
        (partial, own, other, *pieces, cosine, sine, bias),
        [VMEM] * 10,
        (jax.ShapeDtypeStruct((rows, heads * HEAD), BF16), jax.ShapeDtypeStruct((8, HEAD), F32)),
        [pltpu.VMEM((rows, wide // 2), F32), pltpu.VMEM((rows, wide // 2), BF16)],
        8.0,
        mib=20,
    )


def output_kernel(at, *refs):
    attended, blocks, others = refs[:3], refs[3:7], refs[7:11]
    residual, partial, w_far, weights, sems = refs[11:]
    rows, wide = attended[0].shape
    part = wide // 2
    count = weights.shape[0] // 4
    a, b, core = at[AT_X_HI], at[AT_X_LO], at[AT_CORE]
    copies = []
    for two, second in enumerate(OFFSETS):
        for one, first in enumerate(OFFSETS):
            for k, (held, leg_core) in enumerate(((blocks, core), (others, 1 - core))):
                y, z = leg_positions(at, leg_core, first, second)
                column = pl.multiple_of(k * part + z * HEAD, HEAD)
                copies.append(
                    pltpu.make_async_copy(
                        held[two].at[pl.ds(one * count, count)],
                        weights.at[
                            pl.ds(pl.multiple_of(y * count, count), count), pl.ds(column, HEAD)
                        ],
                        sems.at[len(copies)],
                    )
                )
    for copy in copies:
        copy.start()
    for copy in copies:
        copy.wait()

    def held_rows(offset, k):
        chip = (2 * a + b + offset) % 4
        there = core if k == 0 else 1 - core
        row = ((chip % 2 * 2 + there) * 2 + chip // 2) * part
        return weights[pl.ds(pl.multiple_of(row, part), part), :]

    for k in range(2):
        w_far[k * part : (k + 1) * part, :] = held_rows(2, k)
    partial[...] = residual[...].astype(F32)
    for piece, offset in zip(attended, OFFSETS[:3], strict=True):
        for k in range(2):
            partial[...] += jnp.dot(
                piece[:, k * part : (k + 1) * part],
                held_rows(offset, k),
                preferred_element_type=F32,
            )


def output_part(at, attended, blocks, others, residual):
    rows, wide = attended[0].shape
    width = blocks[0].shape[0]
    return call(
        output_kernel,
        (at, *attended, *blocks, *others, residual),
        [SMEM] + [VMEM] * 3 + [HBM] * 8 + [VMEM],
        (jax.ShapeDtypeStruct((rows, wide), F32), jax.ShapeDtypeStruct((wide, wide), BF16)),
        [
            pltpu.VMEM((width, wide), BF16),
            pltpu.SemaphoreType.DMA((32,)),
        ],
        9.5,
        mib=28,
    )


def output_rest_kernel(partial, low, high, w_far, h, square):
    half, wide = low.shape
    for k, piece in enumerate((low, high)):
        at_rows = slice(k * half, (k + 1) * half)
        product = jnp.dot(piece[...], w_far[...], preferred_element_type=F32)
        block = (partial[at_rows, :] + product).astype(BF16)
        h[at_rows, :] = block
        block = block.astype(F32)
        block = block * block
        folded = block[:, :HEAD]
        for lane in range(HEAD, wide, HEAD):
            folded = folded + block[:, lane : lane + HEAD]
        square[:, at_rows] = jnp.sum(folded.T, axis=0, keepdims=True)


def output_rest(partial, w_far, low, high):
    rows, wide = partial.shape
    return call(
        output_rest_kernel,
        (partial, low, high, w_far),
        [VMEM] * 4,
        (jax.ShapeDtypeStruct((rows, wide), BF16), jax.ShapeDtypeStruct((1, rows), F32)),
        [],
        1.5,
        mib=14,
    )


def pool_kernel(width, h, square, packed, packed_other, mask, out):
    rows, wide = h.shape
    entries = packed.shape[0] - 16
    scale = jnp.broadcast_to(lax.rsqrt(square[...] / width + EPS), (HEAD, rows)).T
    keep = jnp.broadcast_to(mask[...], (HEAD, rows)).T
    count = jnp.sum(mask[...], axis=1, keepdims=True)
    heads, tile = wide // HEAD, 256
    for head in range(heads):
        cols = slice(head * HEAD, (head + 1) * HEAD)
        held = packed if head < heads // 2 else packed_other
        start = head % (heads // 2) * HEAD
        gain = held[entries:, start : start + HEAD].astype(F32)[:1]
        block = (h[:, cols].astype(F32) * scale * gain).astype(BF16)
        lat = held[:entries, start : start + HEAD]
        folded = jnp.zeros((entries, HEAD), F32)
        for lo in range(0, rows, tile):
            some = slice(lo, lo + tile)
            logits = lax.dot_general(lat, block[some, :], NT, preferred_element_type=F32)
            top = jnp.max(logits, axis=0, keepdims=True)
            power = jnp.exp2((logits - top) * EXPONENT)
            power = power * (mask[:, some] / jnp.sum(power, axis=0, keepdims=True))
            for k in range(0, tile, HEAD):
                folded = folded + power[:, k : k + HEAD]
        taken = jnp.sum(folded, axis=1, keepdims=True)
        cross = jnp.sum(taken * lat.astype(F32), axis=0, keepdims=True)
        kept = jnp.sum(block.astype(F32) * keep, axis=0, keepdims=True)
        out[:, cols] = (cross + kept) / count


def pool(h, square, packed, packed_other, mask):
    rows, wide = h.shape

    def kernel(*refs):
        pool_kernel(4 * wide, *refs)

    return call(
        kernel,
        (h, square, packed, packed_other, mask),
        [VMEM] * 5,
        jax.ShapeDtypeStruct((1, wide), F32),
        [],
        3.5,
        mib=14,
    )


def turn_kernel(at, queries, out, held, sem):
    count = out.shape[1]
    start = pl.multiple_of(at[0] * count, count)
    copy = pltpu.make_async_copy(queries.at[pl.ds(start, count)], held, sem.at[0])
    copy.start()
    copy.wait()
    out[...] = held[...].T


def turn(at, queries, count):
    part = queries.shape[1]
    return call(
        turn_kernel,
        (at, queries),
        [SMEM, HBM],
        jax.ShapeDtypeStruct((part, count), BF16),
        [pltpu.VMEM((count, part), BF16), pltpu.SemaphoreType.DMA((1,))],
        2.0,
        mib=58,
    )


def score_kernel(every, norms, *refs):
    parts, out = refs[:-1], refs[-1]
    tile = parts[0].shape[1]
    count = tile * len(parts)
    block = every[...]
    values = block.astype(F32)
    square = jnp.sum(values * values, axis=1, keepdims=True)
    out[:, count : count + HEAD] = jnp.broadcast_to(square, (block.shape[0], HEAD))
    out[: norms.shape[0], count + HEAD :] = norms[...]
    out[norms.shape[0] :, count + HEAD :] = jnp.zeros_like(norms)
    for k, held in enumerate(parts):
        out[:, k * tile : (k + 1) * tile] = jnp.dot(
            block, held[...], preferred_element_type=F32
        )


def score(every, norms, parts):
    passages = every.shape[0]
    count = parts[0].shape[1] * len(parts)
    return call(
        score_kernel,
        (every, norms, *parts),
        [VMEM] * (2 + len(parts)),
        jax.ShapeDtypeStruct((passages, count + 2 * HEAD), F32),
        [],
        1.0,
        mib=10,
    )


def merge_kernel(mine, other, out):
    wide = out.shape[1]
    count = wide - 4 * HEAD
    total = mine[...] + other[...]
    rest = total[:, count:]
    high = rest.astype(BF16)
    out[:, :count] = total[:, :count].astype(BF16)
    out[:, count : count + 2 * HEAD] = high
    out[:, count + 2 * HEAD :] = (rest - high.astype(F32)).astype(BF16)


def merge(mine, other):
    passages, wide = mine.shape
    return call(
        merge_kernel,
        (mine, other),
        [VMEM] * 2,
        jax.ShapeDtypeStruct((passages, wide + 2 * HEAD), BF16),
        [],
        0.6,
        mib=6,
    )


def finish_kernel(mine, other, similarity, log_norm):
    count = similarity.shape[1]
    total = mine[...].astype(F32) + other[...].astype(F32)
    rest = total[:, count : count + 2 * HEAD] + total[:, count + 2 * HEAD :]
    scale = lax.rsqrt(rest[:, :1] + 1e-06) / logit_divisor
    norms = [rest[k : k + 1, HEAD:] for k in range(count // HEAD)]
    scores = total[:, :count] * scale * lax.rsqrt(jnp.concatenate(norms, axis=1) + 1e-06)
    similarity[...] = scores
    top = jnp.max(scores, axis=0, keepdims=True)
    log_norm[...] = top + jnp.log(jnp.sum(jnp.exp(scores - top), axis=0, keepdims=True))


def finish(mine, other):
    passages, wide = mine.shape
    count = wide - 4 * HEAD
    return call(
        finish_kernel,
        (mine, other),
        [VMEM] * 2,
        (
            jax.ShapeDtypeStruct((passages, count), F32),
            jax.ShapeDtypeStruct((1, count), F32),
        ),
        [],
        0.8,
        mib=6,
    )


def local(
    hidden_in, norm_gain, w_query, w_key, w_value, w_out, final_gain, latents, token_mask, queries
):
    length, part_width = hidden_in.shape[1:]
    part = part_width // 2
    dp, tensor = lax.axis_index("dp"), lax.axis_index("tensor")
    y, x_hi, z = dp // 8, (dp // 4) % 2, dp % 4
    x_lo, core = tensor // 2, tensor % 2
    at = jnp.stack([y, x_hi, z, x_lo, core]).astype(jnp.int32)

    def halves(side):
        taken = []
        for weights in (w_query, w_key, w_value):
            wide = weights.shape[1] // 2
            taken.append(lax.dynamic_slice_in_dim(weights, side * wide, wide, 1))
        return jnp.concatenate(taken, axis=1)

    half = HEAD // 2
    freqs = 10000.0 ** (-2.0 * jnp.arange(half, dtype=F32) / HEAD)
    angle = jnp.arange(length, dtype=F32)[:, None] * freqs[None, :]
    cosine = jnp.concatenate([jnp.cos(angle), jnp.cos(angle)], axis=1)
    sine = jnp.concatenate([-jnp.sin(angle), jnp.sin(angle)], axis=1)

    hidden = hidden_in[0]
    hidden_other = move(hidden, lambda y, a, z, b, c: (y, a, z, b, a), lambda y, a, z, b, c: c != a)
    whole = jnp.concatenate([hidden, hidden_other], axis=0)
    lat = lax.dynamic_slice_in_dim(latents, x_hi * part, part, 1)
    gain = lax.dynamic_slice_in_dim(final_gain, x_hi * part, part, 0)
    packed = jnp.concatenate([lat, jnp.broadcast_to(gain[None], (16, part))], axis=0)
    packed_other = swap_core(packed)
    q_f = queries.astype(F32)
    norms = jnp.sum(q_f * q_f, -1).reshape(-1, HEAD)

    theirs = halves(1 - x_hi)
    deep, wide = theirs.shape
    row = jnp.pad(token_mask.astype(BF16), ((0, 15), (0, wide - length)))
    theirs = swap_x_hi(jnp.concatenate([theirs, row], axis=0))
    mask_other = theirs[deep : deep + 1, :length].astype(jnp.int32)
    whole = behind(whole, theirs, norms, packed_other)
    x_before = move(whole, along_x(1), holds(0))
    x_after = move(whole, along_x(-1), holds(0))

    shard = jnp.concatenate([halves(x_hi), theirs[:deep]], axis=0)
    shard = behind(shard, norms, packed_other)
    line = jnp.concatenate(direct(shard, first_leg), axis=0)
    w_before, w_after = near(line, second_leg)
    line_other = swap_core(line)
    there = line_other[:1, :1]
    x_low, x_high = halves_of(behind(x_before, there), behind(x_after, there))
    x_low = move(x_low, along_x(1), holds(-1))
    x_high = move(x_high, along_x(-1), holds(1))
    low, high = halves_of(w_before, w_after)
    w_low, w_high = far(low, high, second_leg)
    w_before_other = swap_core(w_before)
    w_after_other = swap_core(w_after)

    own, other, residual, scaled = normalize(
        at, (whole, x_before, x_after, x_low, x_high), norm_gain[None].astype(F32)
    )
    partial = project_part(
        own, other, (line, w_before, w_after), (line_other, w_before_other, w_after_other)
    )

    mask = jnp.where(x_hi == core, token_mask, mask_other)
    bias = jnp.where(mask[0][:, None] > 0, 0.0, -1e30).astype(F32)
    bias = jnp.broadcast_to(bias, (length, HEAD))
    mask = mask.astype(F32)
    w_pieces = (w_low, w_high, swap_core(w_low), swap_core(w_high))
    projected = partial[:1, :1]
    cosine = behind(cosine, projected, scaled)
    attended, seen = attend(partial, own, other, w_pieces, cosine, sine, bias)
    a_before, a_after = near(attended, along_x)

    block = move(behind(w_out, scaled), lambda y, a, z, b, c: (2 * b + c, a, z, y // 2, y % 2))
    out_blocks = direct(behind(block, projected), first_leg)
    out_line = jnp.concatenate([behind(piece, seen) for piece in out_blocks], axis=0)
    out_pieces = direct(out_line, second_leg)
    out_others = tuple(swap_core(piece) for piece in out_pieces)

    a_low, a_high = halves_of(a_before, a_after)
    a_low, a_high = far(a_low, a_high, along_x)
    partial, w_out_far = output_part(
        at,
        (attended, a_before, a_after),
        out_pieces,
        out_others,
        residual,
    )
    h, square = output_rest(partial, w_out_far, a_low, a_high)
    parts = 4
    turned = [
        turn(behind(jnp.full((1,), k, jnp.int32), square), queries, queries.shape[0] // parts)
        for k in range(parts)
    ]
    square = square + swap_x_lo(square)
    square = square + swap_x_next(square)
    pooled = pool(h, square, packed, packed_other, mask)

    def in_order(first, values, other, axis):
        low, high = jnp.where(first, values, other), jnp.where(first, other, values)
        return jnp.concatenate([low, high], axis=axis)

    emb = pooled.astype(BF16)
    emb = in_order(core == 0, emb[:, :part], swap_core(emb[:, part:]), 0)
    emb = in_order(x_hi == 0, emb, swap_x_hi(emb), 1)
    emb = emb[None, :, None]
    emb = in_order(z % 2 == 0, emb, move(emb, lambda y, a, z, b, c: (y, a, z ^ 1, b, c)), 2)
    emb = in_order(z < 2, emb, move(emb, lambda y, a, z, b, c: (y, a, 3 - z, b, c)), 2)
    emb = in_order(y % 2 == 0, emb, move(emb, lambda y, a, z, b, c: (y ^ 1, a, z, b, c)), 0)
    emb = in_order(y < 2, emb, move(emb, lambda y, a, z, b, c: (3 - y, a, z, b, c)), 0)
    products = score(emb.reshape(32, part_width), norms, turned)
    products = merge(products, swap_core(products))
    similarity, log_norm = finish(products, swap_x_lo(products))
    return (similarity.T, log_norm[0])


def solution(mesh):
    placed = (
        P("dp", None, "tensor"),
        P(),
        P("dp", "tensor"),
        P("dp", "tensor"),
        P("dp", "tensor"),
        P("tensor", "dp"),
        P("tensor"),
        P(None, "tensor"),
        P("dp", None),
        P("dp", "tensor"),
    )
    return jax.shard_map(
        local, mesh=mesh, in_specs=placed, out_specs=(P("dp", None), P("dp")), check_vma=False
    )
```

```python
import jax
import jax.numpy as jnp
from jax import lax
from jax.experimental import pallas as pl
from jax.experimental.pallas import tpu as pltpu
from jax.sharding import PartitionSpec as P

HEAD = 128
EPS = 1e-05
logit_divisor = 0.02
BOTH = ("dp", "tensor")
COORDS = [
    (y, a, z, b, c)
    for y in range(4)
    for a in range(2)
    for z in range(4)
    for b in range(2)
    for c in range(2)
]


def index_of(y, a, z, b, c):
    return (((y * 2 + a) * 4 + z) * 2 + b) * 2 + c


def move(values, where, when=lambda *at: True):
    pairs = [(index_of(*at), index_of(*where(*at))) for at in COORDS if when(*at)]
    return lax.ppermute(values, BOTH, pairs)


def swap_core(values):
    return move(values, lambda y, a, z, b, c: (y, a, z, b, 1 - c))


def swap_x_hi(values):
    return move(values, lambda y, a, z, b, c: (y, 1 - a, z, b, c))


def swap_x_lo(values):
    return move(values, lambda y, a, z, b, c: (y, a, z, 1 - b, c))


def swap_x_next(values):
    return move(values, lambda y, a, z, b, c: (y, 1 - a, z, 1 - b, c))


def along_x(step):
    def where(y, a, z, b, c):
        x = (2 * a + b + step) % 4
        return (y, x // 2, z, x % 2, c)

    return where


def first_leg(step):
    def where(y, a, z, b, c):
        if c == 0:
            return ((y + step) % 4, a, z, b, c)
        return (y, a, (z + step) % 4, b, c)

    return where


def second_leg(step):
    def where(y, a, z, b, c):
        if c == 0:
            return (y, a, (z + step) % 4, b, c)
        return ((y + step) % 4, a, z, b, c)

    return where


def near(values, leg):
    return move(values, leg(1)), move(values, leg(-1))


def halves_of(before, after):
    half = before.shape[0] // 2
    return before[:half], after[half:]


def far(low, high, leg):
    return move(low, leg(1)), move(high, leg(-1))


def direct(values, leg):
    return values, move(values, leg(1)), move(values, leg(-1)), move(values, leg(2))


def holds(step):
    def when(y, a, z, b, c):
        return (2 * a + b + step) % 4 // 2 == c

    return when


def behind(values, *others):
    return lax.optimization_barrier((values,) + others)[0]


AT_Y, AT_X_HI, AT_Z, AT_X_LO, AT_CORE = range(5)
VMEM = pl.BlockSpec(memory_space=pltpu.VMEM)
SMEM = pl.BlockSpec(memory_space=pltpu.SMEM)
HBM = pl.BlockSpec(memory_space=pltpu.HBM)
F32, BF16 = jnp.float32, jnp.bfloat16
OFFSETS = (0, 3, 1, 2)
NT = (((1,), (1,)), ((), ()))
RATE = 1.15e9
EXPONENT = HEAD ** (-0.5) * 1.4426950408889634


def call(kernel, args, specs, out, scratch, micros, mib=48):
    return pl.pallas_call(
        kernel,
        out_shape=out,
        in_specs=specs,
        out_specs=jax.tree.map(lambda _: VMEM, out),
        scratch_shapes=scratch,
        compiler_params=pltpu.CompilerParams(vmem_limit_bytes=mib * 1024 * 1024),
        cost_estimate=pl.CostEstimate(
            flops=int(micros * RATE), bytes_accessed=1024, transcendentals=0
        ),
    )(*args)


def leg_positions(at, core, first, second):
    y = jnp.where(core == 0, at[AT_Y] + first, at[AT_Y] + second) % 4
    z = jnp.where(core == 0, at[AT_Z] + second, at[AT_Z] + first) % 4
    return y, z


def norm_kernel(at, *refs):
    whole, before, after, low, high, gain, own, other, residual, done, tokens, sems = refs
    rows, part = low.shape
    done[...] = jnp.zeros_like(done)
    a, b, core = at[AT_X_HI], at[AT_X_LO], at[AT_CORE]
    here = a == core
    near = jnp.logical_or(
        jnp.logical_and(here, b == 0), jnp.logical_and(jnp.logical_not(here), b == 1)
    )

    def send(src, block, sem):
        column = pl.multiple_of(block * part, part)
        return pltpu.make_async_copy(src, tokens.at[:, pl.ds(column, part)], sems.at[sem])

    first, second = 2 * b + core, 2 * b + 1 - core
    third, fourth = 2 * (1 - b) + core, 2 * (1 - b) + 1 - core

    @pl.when(here)
    def _():
        send(whole.at[pl.ds(0, rows)], first, 0).start()
        send(whole.at[pl.ds(rows, rows)], second, 1).start()

    @pl.when(jnp.logical_not(here))
    def _():
        send(low, first, 0).start()
        send(high, second, 1).start()

    @pl.when(near)
    def _():
        send(after.at[pl.ds(0, rows)], third, 2).start()
        send(after.at[pl.ds(rows, rows)], fourth, 3).start()

    @pl.when(jnp.logical_not(near))
    def _():
        send(before.at[pl.ds(0, rows)], third, 2).start()
        send(before.at[pl.ds(rows, rows)], fourth, 3).start()

    for sem in range(4):
        send(low, 0, sem).wait()

    own_columns = part // 2
    for k, held in enumerate((first, second)):
        lane = pl.multiple_of(held * part + a * own_columns, own_columns)
        residual[:, k * own_columns : (k + 1) * own_columns] = tokens[:, pl.ds(lane, own_columns)]

    width = tokens.shape[1]
    tile = 128
    lanes = []
    for two, later in enumerate(OFFSETS):
        for one, sooner in enumerate(OFFSETS):
            y, z = leg_positions(at, core, sooner, later)
            for entry in range(2):
                lane = pl.multiple_of((y * 8 + (a + entry) % 2 * 4 + z) * HEAD, HEAD)
                mine = ((two * 4 + one) * 2 + entry) * HEAD
                turned = ((one * 4 + two) * 2 + entry) * HEAD
                lanes.append((pl.ds(lane, HEAD), mine, turned))

    @pl.loop(0, rows // tile)
    def _(step):
        at_rows = pl.ds(pl.multiple_of(step * tile, tile), tile)
        squares = jnp.zeros((tile, HEAD), F32)
        for lane in range(0, width, HEAD):
            values = tokens[at_rows, lane : lane + HEAD].astype(F32)
            squares = squares + values * values
        mean = jnp.sum(squares, axis=-1, keepdims=True) / width
        scale = jnp.broadcast_to(lax.rsqrt(mean + EPS), (tile, HEAD))
        for lane, mine, turned in lanes:
            values = tokens[at_rows, lane].astype(F32) * scale * gain[:, lane]
            values = values.astype(BF16)
            own[at_rows, mine : mine + HEAD] = values
            other[at_rows, turned : turned + HEAD] = values


def normalize(at, hidden, gain):
    rows, part = hidden[3].shape
    width = gain.shape[1]
    return call(
        norm_kernel,
        (at, *hidden, gain),
        [SMEM] + [HBM] * 5 + [VMEM],
        (
            jax.ShapeDtypeStruct((rows, width), BF16),
            jax.ShapeDtypeStruct((rows, width), BF16),
            jax.ShapeDtypeStruct((rows, part), BF16),
            jax.ShapeDtypeStruct((8, HEAD), F32),
        ),
        [pltpu.VMEM((rows, width), BF16), pltpu.SemaphoreType.DMA((4,))],
        30.0,
        mib=16,
    )


def project_kernel(own, other, *refs):
    lines, total = refs[:6], refs[6]
    deep, wide = lines[0].shape
    for k, normed in enumerate((own, other)):
        total[:, k * wide : (k + 1) * wide] = sum(
            jnp.dot(
                normed[:, j * deep : (j + 1) * deep],
                lines[3 * k + j][...],
                preferred_element_type=F32,
            )
            for j in range(3)
        )


def project_part(own, other, lines, others):
    rows = own.shape[0]
    wide = lines[0].shape[1]
    return call(
        project_kernel,
        (own, other, *lines, *others),
        [VMEM] * 8,
        jax.ShapeDtypeStruct((rows, 2 * wide), F32),
        [],
        7.0,
        mib=20,
    )


def attention_kernel(partial, own, other, *refs):
    pieces, (cosine, sine, bias, out, done, total, qkv) = refs[:4], refs[4:]
    done[...] = jnp.zeros_like(done)
    rows = partial.shape[0]
    half = pieces[0].shape[0]
    wide = partial.shape[1] // 2
    heads = wide // HEAD - 2
    for k, normed in enumerate((own, other)):
        base = k * wide
        start = normed.shape[1] - 2 * half
        total[...] = (
            partial[:, base : base + wide]
            + jnp.dot(
                normed[:, start : start + half], pieces[2 * k][...], preferred_element_type=F32
            )
            + jnp.dot(
                normed[:, start + half :], pieces[2 * k + 1][...], preferred_element_type=F32
            )
        )
        for head in range(heads + 1):
            cols = slice(head * HEAD, (head + 1) * HEAD)
            block = total[:, cols]
            turned = block * cosine[...] + pltpu.roll(block, HEAD // 2, 1) * sine[...]
            qkv[:, cols] = turned.astype(BF16)
        keys = qkv[:, heads * HEAD : (heads + 1) * HEAD]
        values_t = total[:, (heads + 1) * HEAD :].T.astype(BF16)
        for head in range(heads):
            query = qkv[:, head * HEAD : (head + 1) * HEAD]
            logits = lax.dot_general(keys, query, NT, preferred_element_type=F32)
            logits = logits + jnp.concatenate([bias[...]] * (rows // HEAD), axis=1)
            top = jnp.max(logits, axis=0, keepdims=True)
            power = jnp.exp2((logits - top) * EXPONENT)
            share = 1.0 / jnp.sum(power, axis=0, keepdims=True)
            mixed = jnp.dot(values_t, power.astype(BF16), preferred_element_type=F32)
            start = (k * heads + head) * HEAD
            out[:, start : start + HEAD] = (mixed * share).T.astype(BF16)


def attend(partial, own, other, pieces, cosine, sine, bias):
    rows, wide = partial.shape
    heads = wide // HEAD - 4
    return call(
        attention_kernel,
        (partial, own, other, *pieces, cosine, sine, bias),
        [VMEM] * 10,
        (jax.ShapeDtypeStruct((rows, heads * HEAD), BF16), jax.ShapeDtypeStruct((8, HEAD), F32)),
        [pltpu.VMEM((rows, wide // 2), F32), pltpu.VMEM((rows, wide // 2), BF16)],
        8.0,
        mib=20,
    )


def output_kernel(at, *refs):
    attended, blocks, others = refs[:3], refs[3:7], refs[7:11]
    residual, partial, w_far, weights, sems = refs[11:]
    rows, wide = attended[0].shape
    part = wide // 2
    count = weights.shape[0] // 4
    a, b, core = at[AT_X_HI], at[AT_X_LO], at[AT_CORE]
    copies = []
    for two, second in enumerate(OFFSETS):
        for one, first in enumerate(OFFSETS):
            for k, (held, leg_core) in enumerate(((blocks, core), (others, 1 - core))):
                y, z = leg_positions(at, leg_core, first, second)
                column = pl.multiple_of(k * part + z * HEAD, HEAD)
                copies.append(
                    pltpu.make_async_copy(
                        held[two].at[pl.ds(one * count, count)],
                        weights.at[
                            pl.ds(pl.multiple_of(y * count, count), count), pl.ds(column, HEAD)
                        ],
                        sems.at[len(copies)],
                    )
                )
    for copy in copies:
        copy.start()
    for copy in copies:
        copy.wait()

    def held_rows(offset, k):
        chip = (2 * a + b + offset) % 4
        there = core if k == 0 else 1 - core
        row = ((chip % 2 * 2 + there) * 2 + chip // 2) * part
        return weights[pl.ds(pl.multiple_of(row, part), part), :]

    for k in range(2):
        w_far[k * part : (k + 1) * part, :] = held_rows(2, k)
    partial[...] = residual[...].astype(F32)
    for piece, offset in zip(attended, OFFSETS[:3], strict=True):
        for k in range(2):
            partial[...] += jnp.dot(
                piece[:, k * part : (k + 1) * part],
                held_rows(offset, k),
                preferred_element_type=F32,
            )


def output_part(at, attended, blocks, others, residual):
    rows, wide = attended[0].shape
    width = blocks[0].shape[0]
    return call(
        output_kernel,
        (at, *attended, *blocks, *others, residual),
        [SMEM] + [VMEM] * 3 + [HBM] * 8 + [VMEM],
        (jax.ShapeDtypeStruct((rows, wide), F32), jax.ShapeDtypeStruct((wide, wide), BF16)),
        [
            pltpu.VMEM((width, wide), BF16),
            pltpu.SemaphoreType.DMA((32,)),
        ],
        9.5,
        mib=28,
    )


def output_rest_kernel(partial, low, high, w_far, h, square):
    half, wide = low.shape
    for k, piece in enumerate((low, high)):
        at_rows = slice(k * half, (k + 1) * half)
        product = jnp.dot(piece[...], w_far[...], preferred_element_type=F32)
        block = (partial[at_rows, :] + product).astype(BF16)
        h[at_rows, :] = block
        block = block.astype(F32)
        block = block * block
        folded = block[:, :HEAD]
        for lane in range(HEAD, wide, HEAD):
            folded = folded + block[:, lane : lane + HEAD]
        square[:, at_rows] = jnp.sum(folded.T, axis=0, keepdims=True)


def output_rest(partial, w_far, low, high):
    rows, wide = partial.shape
    return call(
        output_rest_kernel,
        (partial, low, high, w_far),
        [VMEM] * 4,
        (jax.ShapeDtypeStruct((rows, wide), BF16), jax.ShapeDtypeStruct((1, rows), F32)),
        [],
        1.5,
        mib=14,
    )


def pool_kernel(width, h, square, packed, packed_other, mask, out):
    rows, wide = h.shape
    entries = packed.shape[0] - 16
    scale = jnp.broadcast_to(lax.rsqrt(square[...] / width + EPS), (HEAD, rows)).T
    keep = jnp.broadcast_to(mask[...], (HEAD, rows)).T
    count = jnp.sum(mask[...], axis=1, keepdims=True)
    heads, tile = wide // HEAD, 256
    for head in range(heads):
        cols = slice(head * HEAD, (head + 1) * HEAD)
        held = packed if head < heads // 2 else packed_other
        start = head % (heads // 2) * HEAD
        gain = held[entries:, start : start + HEAD].astype(F32)[:1]
        block = (h[:, cols].astype(F32) * scale * gain).astype(BF16)
        lat = held[:entries, start : start + HEAD]
        folded = jnp.zeros((entries, HEAD), F32)
        for lo in range(0, rows, tile):
            some = slice(lo, lo + tile)
            logits = lax.dot_general(lat, block[some, :], NT, preferred_element_type=F32)
            top = jnp.max(logits, axis=0, keepdims=True)
            power = jnp.exp2((logits - top) * EXPONENT)
            power = power * (mask[:, some] / jnp.sum(power, axis=0, keepdims=True))
            for k in range(0, tile, HEAD):
                folded = folded + power[:, k : k + HEAD]
        taken = jnp.sum(folded, axis=1, keepdims=True)
        cross = jnp.sum(taken * lat.astype(F32), axis=0, keepdims=True)
        kept = jnp.sum(block.astype(F32) * keep, axis=0, keepdims=True)
        out[:, cols] = (cross + kept) / count


def pool(h, square, packed, packed_other, mask):
    rows, wide = h.shape

    def kernel(*refs):
        pool_kernel(4 * wide, *refs)

    return call(
        kernel,
        (h, square, packed, packed_other, mask),
        [VMEM] * 5,
        jax.ShapeDtypeStruct((1, wide), F32),
        [],
        3.5,
        mib=14,
    )


def turn_kernel(at, queries, out, held, sem):
    count = out.shape[1]
    start = pl.multiple_of(at[0] * count, count)
    copy = pltpu.make_async_copy(queries.at[pl.ds(start, count)], held, sem.at[0])
    copy.start()
    copy.wait()
    out[...] = held[...].T


def turn(at, queries, count):
    part = queries.shape[1]
    return call(
        turn_kernel,
        (at, queries),
        [SMEM, HBM],
        jax.ShapeDtypeStruct((part, count), BF16),
        [pltpu.VMEM((count, part), BF16), pltpu.SemaphoreType.DMA((1,))],
        2.0,
        mib=58,
    )


def score_kernel(every, norms, *refs):
    parts, out = refs[:-1], refs[-1]
    tile = parts[0].shape[1]
    count = tile * len(parts)
    block = every[...]
    values = block.astype(F32)
    square = jnp.sum(values * values, axis=1, keepdims=True)
    out[:, count : count + HEAD] = jnp.broadcast_to(square, (block.shape[0], HEAD))
    out[: norms.shape[0], count + HEAD :] = norms[...]
    out[norms.shape[0] :, count + HEAD :] = jnp.zeros_like(norms)
    for k, held in enumerate(parts):
        out[:, k * tile : (k + 1) * tile] = jnp.dot(
            block, held[...], preferred_element_type=F32
        )


def score(every, norms, parts):
    passages = every.shape[0]
    count = parts[0].shape[1] * len(parts)
    return call(
        score_kernel,
        (every, norms, *parts),
        [VMEM] * (2 + len(parts)),
        jax.ShapeDtypeStruct((passages, count + 2 * HEAD), F32),
        [],
        1.0,
        mib=10,
    )


def merge_kernel(mine, other, out):
    wide = out.shape[1]
    count = wide - 4 * HEAD
    total = mine[...] + other[...]
    rest = total[:, count:]
    high = rest.astype(BF16)
    out[:, :count] = total[:, :count].astype(BF16)
    out[:, count : count + 2 * HEAD] = high
    out[:, count + 2 * HEAD :] = (rest - high.astype(F32)).astype(BF16)


def merge(mine, other):
    passages, wide = mine.shape
    return call(
        merge_kernel,
        (mine, other),
        [VMEM] * 2,
        jax.ShapeDtypeStruct((passages, wide + 2 * HEAD), BF16),
        [],
        0.6,
        mib=6,
    )


def finish_kernel(mine, other, similarity, log_norm):
    count = similarity.shape[1]
    total = mine[...].astype(F32) + other[...].astype(F32)
    rest = total[:, count : count + 2 * HEAD] + total[:, count + 2 * HEAD :]
    scale = lax.rsqrt(rest[:, :1] + 1e-06) / logit_divisor
    norms = [rest[k : k + 1, HEAD:] for k in range(count // HEAD)]
    scores = total[:, :count] * scale * lax.rsqrt(jnp.concatenate(norms, axis=1) + 1e-06)
    similarity[...] = scores
    top = jnp.max(scores, axis=0, keepdims=True)
    log_norm[...] = top + jnp.log(jnp.sum(jnp.exp(scores - top), axis=0, keepdims=True))


def finish(mine, other):
    passages, wide = mine.shape
    count = wide - 4 * HEAD
    return call(
        finish_kernel,
        (mine, other),
        [VMEM] * 2,
        (
            jax.ShapeDtypeStruct((passages, count), F32),
            jax.ShapeDtypeStruct((1, count), F32),
        ),
        [],
        0.8,
        mib=6,
    )


def local(
    hidden_in, norm_gain, w_query, w_key, w_value, w_out, final_gain, latents, token_mask, queries
):
    length, part_width = hidden_in.shape[1:]
    part = part_width // 2
    dp, tensor = lax.axis_index("dp"), lax.axis_index("tensor")
    y, x_hi, z = dp // 8, (dp // 4) % 2, dp % 4
    x_lo, core = tensor // 2, tensor % 2
    at = jnp.stack([y, x_hi, z, x_lo, core]).astype(jnp.int32)

    def halves(side):
        taken = []
        for weights in (w_query, w_key, w_value):
            wide = weights.shape[1] // 2
            taken.append(lax.dynamic_slice_in_dim(weights, side * wide, wide, 1))
        return jnp.concatenate(taken, axis=1)

    half = HEAD // 2
    freqs = 10000.0 ** (-2.0 * jnp.arange(half, dtype=F32) / HEAD)
    angle = jnp.arange(length, dtype=F32)[:, None] * freqs[None, :]
    cosine = jnp.concatenate([jnp.cos(angle), jnp.cos(angle)], axis=1)
    sine = jnp.concatenate([-jnp.sin(angle), jnp.sin(angle)], axis=1)

    hidden = hidden_in[0]
    hidden_other = move(hidden, lambda y, a, z, b, c: (y, a, z, b, a), lambda y, a, z, b, c: c != a)
    whole = jnp.concatenate([hidden, hidden_other], axis=0)
    lat = lax.dynamic_slice_in_dim(latents, x_hi * part, part, 1)
    gain = lax.dynamic_slice_in_dim(final_gain, x_hi * part, part, 0)
    packed = jnp.concatenate([lat, jnp.broadcast_to(gain[None], (16, part))], axis=0)
    packed_other = swap_core(packed)
    q_f = queries.astype(F32)
    norms = jnp.sum(q_f * q_f, -1).reshape(-1, HEAD)

    theirs = halves(1 - x_hi)
    deep, wide = theirs.shape
    row = jnp.pad(token_mask.astype(BF16), ((0, 15), (0, wide - length)))
    theirs = swap_x_hi(jnp.concatenate([theirs, row], axis=0))
    mask_other = theirs[deep : deep + 1, :length].astype(jnp.int32)
    whole = behind(whole, theirs, norms, packed_other)
    x_before = move(whole, along_x(1), holds(0))
    x_after = move(whole, along_x(-1), holds(0))

    shard = jnp.concatenate([halves(x_hi), theirs[:deep]], axis=0)
    shard = behind(shard, norms, packed_other)
    line = jnp.concatenate(direct(shard, first_leg), axis=0)
    w_before, w_after = near(line, second_leg)
    line_other = swap_core(line)
    there = line_other[:1, :1]
    x_low, x_high = halves_of(behind(x_before, there), behind(x_after, there))
    x_low = move(x_low, along_x(1), holds(-1))
    x_high = move(x_high, along_x(-1), holds(1))
    low, high = halves_of(w_before, w_after)
    w_low, w_high = far(low, high, second_leg)
    w_before_other = swap_core(w_before)
    w_after_other = swap_core(w_after)

    own, other, residual, scaled = normalize(
        at, (whole, x_before, x_after, x_low, x_high), norm_gain[None].astype(F32)
    )
    partial = project_part(
        own, other, (line, w_before, w_after), (line_other, w_before_other, w_after_other)
    )

    mask = jnp.where(x_hi == core, token_mask, mask_other)
    bias = jnp.where(mask[0][:, None] > 0, 0.0, -1e30).astype(F32)
    bias = jnp.broadcast_to(bias, (length, HEAD))
    mask = mask.astype(F32)
    w_pieces = (w_low, w_high, swap_core(w_low), swap_core(w_high))
    projected = partial[:1, :1]
    cosine = behind(cosine, projected, scaled)
    attended, seen = attend(partial, own, other, w_pieces, cosine, sine, bias)
    a_before, a_after = near(attended, along_x)

    block = move(behind(w_out, scaled), lambda y, a, z, b, c: (2 * b + c, a, z, y // 2, y % 2))
    block = behind(block, projected)
    out_before, out_after = near(block, first_leg)
    out_blocks = (block, out_before, out_after, move(behind(out_before, seen), first_leg(1)))
    out_line = jnp.concatenate([behind(piece, seen) for piece in out_blocks], axis=0)
    out_pieces = direct(out_line, second_leg)
    out_others = tuple(swap_core(piece) for piece in out_pieces)

    a_low, a_high = halves_of(a_before, a_after)
    a_low, a_high = far(a_low, a_high, along_x)
    partial, w_out_far = output_part(
        at,
        (attended, a_before, a_after),
        out_pieces,
        out_others,
        residual,
    )
    h, square = output_rest(partial, w_out_far, a_low, a_high)
    parts = 4
    turned = [
        turn(behind(jnp.full((1,), k, jnp.int32), square), queries, queries.shape[0] // parts)
        for k in range(parts)
    ]
    square = square + swap_x_lo(square)
    square = square + swap_x_next(square)
    pooled = pool(h, square, packed, packed_other, mask)

    def in_order(first, values, other, axis):
        low, high = jnp.where(first, values, other), jnp.where(first, other, values)
        return jnp.concatenate([low, high], axis=axis)

    emb = pooled.astype(BF16)
    emb = in_order(core == 0, emb[:, :part], swap_core(emb[:, part:]), 0)
    emb = in_order(x_hi == 0, emb, swap_x_hi(emb), 1)
    emb = emb[None, :, None]
    emb = in_order(z % 2 == 0, emb, move(emb, lambda y, a, z, b, c: (y, a, z ^ 1, b, c)), 2)
    emb = in_order(z < 2, emb, move(emb, lambda y, a, z, b, c: (y, a, 3 - z, b, c)), 2)
    emb = in_order(y % 2 == 0, emb, move(emb, lambda y, a, z, b, c: (y ^ 1, a, z, b, c)), 0)
    emb = in_order(y < 2, emb, move(emb, lambda y, a, z, b, c: (3 - y, a, z, b, c)), 0)
    products = score(emb.reshape(32, part_width), norms, turned)
    products = merge(products, swap_core(products))
    similarity, log_norm = finish(products, swap_x_lo(products))
    return (similarity.T, log_norm[0])


def solution(mesh):
    placed = (
        P("dp", None, "tensor"),
        P(),
        P("dp", "tensor"),
        P("dp", "tensor"),
        P("dp", "tensor"),
        P("tensor", "dp"),
        P("tensor"),
        P(None, "tensor"),
        P("dp", None),
        P("dp", "tensor"),
    )
    return jax.shard_map(
        local, mesh=mesh, in_specs=placed, out_specs=(P("dp", None), P("dp")), check_vma=False
    )
```
